256 devices in a mesh: gx: 4 (over x), gy: 8 (over z), gz: 8 (over y, core).
Axes of the slice: x: 4, y: 4, z: 8, core: 2. Of those that a mesh axis runs over, the one named last changes fastest.
Arguments:
- right_side: float32 [64, 256, 1024], P('gx', 'gy', 'gz'), may hold values from -4 to 4
- coefficient: float32 [64, 256, 1024], P('gx', 'gy', 'gz'), may hold values from 0.25 to 4
- guess: float32 [64, 256, 1024], P('gx', 'gy', 'gz'), may hold values from -6 to 6
Outputs:
- iterate: float32 [64, 256, 1024], P('gx', 'gy', 'gz')
The draws below stay inside these ranges and needn't reach their ends.
All inputs are finite; a program needn't handle non-finite values.
Results may differ from the reference program's by a relative error of at most 0.0001.
Values sent between devices are 32-bit elements; how exact they have to be, the bound alone decides.
A program may use at most 128 MiB of HBM per device.

```python
import math
import jax
import jax.numpy as jnp
from jax import lax

SWEEPS = 2
CHEB = 20
NX = 64
NY = 256
NZ = 1024


def draw_right_side(key, part):
    key = jax.random.fold_in(key, 11)
    return jnp.clip(jax.random.normal(key, (NX, NY, NZ), jnp.float32), -4.0, 4.0)


def shard_levels(rng, shape, cuts, low, high):
    gain = 1.0
    for axis_at, blocks in cuts:
        draws = jax.random.uniform(jax.random.fold_in(jax.random.fold_in(rng, 6), axis_at), (blocks,), jnp.float32, low / len(cuts), high / len(cuts))
        gain = gain * jnp.repeat(jnp.exp(draws), shape[axis_at] // blocks).reshape((-1,) + (1,) * (len(shape) - 1 - axis_at))
    return gain


def centred(rng, shape, width, reach, pieces=(), kind=jnp.bfloat16):
    gain = shard_levels(rng, shape, pieces, -0.22, 0.18) if pieces else 1.0
    array = jax.random.normal(rng, shape, jnp.float32) * width * gain
    return jnp.minimum(jnp.maximum(array, -reach), reach).astype(kind)


def setup_inputs(seed: int = 0) -> dict:
    streams_of = jax.random.split(jax.random.key(seed), 4)
    return {
        "right_side": draw_right_side(jax.random.fold_in(streams_of[3], 71), 0),
        "coefficient": jnp.clip(jnp.exp(math.log(4.0) - 2.7725887 * jax.random.uniform(streams_of[1], (NX, NY, NZ), jnp.float32) ** shard_levels(streams_of[1], (NX, NY, NZ), ((0, 4), (1, 8), (2, 8)), -0.2, 0.2)), 0.25, 4.0),
        "guess": centred(streams_of[2], (NX, NY, NZ), 1.0, 6.0, ((0, 4), (1, 8), (2, 8)), jnp.float32),
    }


OMEGA = 2.0 / 3.0
CHEB_LOW = 0.1
CHEB_HIGH = 2.0
OFFSETS = ((2, 1, 1), (0, 1, 1), (1, 2, 1), (1, 0, 1), (1, 1, 2), (1, 1, 0))


def restrict(field):
    size_x, size_y, size_z = field.shape
    return field.reshape(size_x // 2, 2, size_y // 2, 2, size_z // 2, 2).mean(axis=(1, 3, 5))


def prolong(field):
    return jnp.repeat(jnp.repeat(jnp.repeat(field, 2, axis=0), 2, axis=1), 2, axis=2)


def neighbour(padded, offset):
    return padded[offset[0]:offset[0] + padded.shape[0] - 2, offset[1]:offset[1] + padded.shape[1] - 2, offset[2]:offset[2] + padded.shape[2] - 2]


def diagonal(padded_coef, scale):
    centre = padded_coef[1:-1, 1:-1, 1:-1]
    total = jnp.zeros_like(centre)
    for offset in OFFSETS:
        total = total + 0.5 * (centre + neighbour(padded_coef, offset))
    return scale * total


def operate(padded_field, padded_coef, scale):
    centre = padded_coef[1:-1, 1:-1, 1:-1]
    value = padded_field[1:-1, 1:-1, 1:-1]
    total = jnp.zeros_like(value)
    for offset in OFFSETS:
        total = total + 0.5 * (centre + neighbour(padded_coef, offset)) * (value - neighbour(padded_field, offset))
    return scale * total


def smooth_once(field, target, padded_coef, diag, scale):
    return field + OMEGA * (target - operate(jnp.pad(field, 1), padded_coef, scale)) / diag


def chebyshev(target, coef, scale):
    padded_coef = jnp.pad(coef, 1)
    diag = diagonal(padded_coef, scale)
    theta = 0.5 * (CHEB_HIGH + CHEB_LOW)
    delta = 0.5 * (CHEB_HIGH - CHEB_LOW)
    sigma = theta / delta
    step = target / diag / theta
    rho = jnp.float32(1.0 / sigma)

    def update(count, carry):
        solution, step, rho = carry
        resid = target - operate(jnp.pad(solution, 1), padded_coef, scale)
        rho_next = 1.0 / (2.0 * sigma - rho)
        step = rho_next * rho * step + (2.0 * rho_next / delta) * resid / diag
        return solution + step, step, rho_next

    solution, step, rho = lax.fori_loop(0, CHEB - 1, update, (step, step, rho))
    return solution


def reference(right_side, coefficient, guess):
    scales = (1.0, 0.25, 0.0625, 0.015625)
    coefs = [coefficient]
    for level in range(3):
        coefs.append(restrict(coefs[-1]))
    padded = [jnp.pad(item, 1) for item in coefs]
    diags = [diagonal(padded[level], scales[level]) for level in range(3)]
    field = guess
    for sweep in range(SWEEPS):
        field = smooth_once(field, right_side, padded[0], diags[0], scales[0])
    targets = [right_side]
    targets.append(restrict(right_side - operate(jnp.pad(field, 1), padded[0], scales[0])))
    errors = [None]
    for level in (1, 2):
        error = OMEGA * targets[level] / diags[level]
        for sweep in range(SWEEPS - 1):
            error = smooth_once(error, targets[level], padded[level], diags[level], scales[level])
        errors.append(error)
        targets.append(restrict(targets[level] - operate(jnp.pad(error, 1), padded[level], scales[level])))
    coarse = chebyshev(targets[3], coefs[3], scales[3])
    for level in (2, 1):
        error = errors[level] + prolong(coarse)
        for sweep in range(SWEEPS):
            error = smooth_once(error, targets[level], padded[level], diags[level], scales[level])
        coarse = error
    field = field + prolong(coarse)
    for sweep in range(SWEEPS):
        field = smooth_once(field, right_side, padded[0], diags[0], scales[0])
    return field
```

```python
import itertools

import jax
import jax.numpy as jnp
import numpy as np
from jax import lax
from jax.experimental import pallas as pl
from jax.experimental.pallas import tpu as pltpu
from jax.sharding import PartitionSpec as P

CHEB = 20
OMEGA = 2.0 / 3.0
CHEB_LOW = 0.1
CHEB_HIGH = 2.0
MESH = pl.DeviceIdType.MESH
F32 = jnp.float32
NX, NY, NZ = 4, 8, 8
SIX = ((1, 0, 0), (-1, 0, 0), (0, 1, 0), (0, -1, 0), (0, 0, 1), (0, 0, -1))
AROUND = sorted(
    (o for o in itertools.product((-1, 0, 1), repeat=3) if o != (0, 0, 0)),
    key=lambda o: -(abs(o[0]) + abs(o[1]) + abs(o[2])),
)
WIDE = sorted(
    (o for o in itertools.product(range(NX), (-1, 0, 1), (-1, 0, 1)) if o != (0, 0, 0)),
    key=lambda o: -((o[0] != 0) + (o[0] == 2) + abs(o[1]) + abs(o[2])),
)


def side(d):
    return 0 if d < 0 else 1


def constants():
    theta, delta = 0.5 * (CHEB_HIGH + CHEB_LOW), 0.5 * (CHEB_HIGH - CHEB_LOW)
    sigma = theta / delta
    rho, out = np.float32(1.0 / sigma), []
    for _ in range(CHEB - 1):
        rho_next = np.float32(1.0 / (2.0 * sigma - rho))
        out += [np.float32(rho_next * rho), np.float32(2.0 * rho_next / delta)]
        rho = rho_next
    return np.array(out, np.float32), theta


def lane(shape):
    return lax.broadcasted_iota(jnp.int32, shape, len(shape) - 1)


def roll(x, by):
    return pltpu.roll(x, by % 128, x.ndim - 1)


def mm(x, m):
    return lax.dot_general(
        x, m, (((1,), (0,)), ((), ())), precision=lax.Precision.HIGHEST, preferred_element_type=F32
    )


def picks(condition, width=128, value=1.0):
    row = lax.broadcasted_iota(jnp.int32, (128, width), 0)
    col = lax.broadcasted_iota(jnp.int32, (128, width), 1)
    return jnp.where(condition(row, col), F32(value), F32(0.0))


def vm(*shape):
    return pltpu.VMEM(shape, F32)


def dma(*shape):
    return pltpu.SemaphoreType.DMA(shape)


def build_scratch():
    s = {}
    for name in ("C0", "V0", "V1", "X0", "VP", "VQ"):
        s[name] = vm(18, 48, 128)
    s.update(WX0=vm(17, 32, 128), WY0=vm(16, 40, 128))
    for name in ("WZM0", "WZP0", "D0", "SD0"):
        s[name] = vm(16, 32, 128)
    s.update(
        YB=vm(5, 2, 16, 1, 128), PZ=vm(5, 32, 128),
        RX=vm(5, 2, 32, 128), RY=vm(5, 2, 16, 1, 128), RZ=vm(5, 2, 32, 128), MZ=vm(5, 32, 128),
        ss0=dma(5, 6), rs0=dma(5, 6),
    )
    s.update(RS0=vm(8, 32, 128), RS1=vm(4, 24, 128), RS2=vm(8, 8, 128), QS=vm(4, 8, 128))
    for k, h in (("c", 5), ("g", 4)):
        s["B1" + k] = vm(8, 16, 128)
        s["PZ1" + k] = vm(16, 128)
        s["RX1" + k] = vm(2, h, 16, 128)
        s["RY1" + k] = vm(2, 8, 8, 128)
        s["RE1" + k] = vm(2, 2, h, 8, 128)
        s["RZ1" + k] = vm(2, 3, 3, 16, 128)
        s["ss1" + k], s["rs1" + k] = dma(26), dma(26)
        s["ZS" + k] = vm(3, 40, 128)
        s["PB2" + k] = vm(8, 128)
        s["S2" + k] = vm(NX, 3, 3, 8, 128)
        s["ss2" + k], s["rs2" + k] = dma(len(WIDE)), dma(len(WIDE))
        s["PB3" + k] = vm(8, 128)
        s["S3" + k] = vm(NZ, 8, 128)
        s["YS" + k] = vm(8, 4, 128)
        s["S4" + k] = vm(NY, 8, 4, 128)
        s["ss3" + k], s["rs3" + k] = dma(NZ), dma(NZ)
        s["ss4" + k], s["rs4" + k] = dma(NY), dma(NY)
    for l in ("1", "2"):
        for name in ("C", "G", "EA", "EB"):
            s[name + l] = vm(18, 40, 128)
        s.update({"WX" + l: vm(17, 24, 128), "WY" + l: vm(16, 32, 128)})
        for name in ("WZM", "WZP", "D", "SD"):
            s[name + l] = vm(16, 24, 128)
    s.update(U2=vm(20, 24, 128), T21=vm(8, 24, 128), D21=vm(8, 24, 128))
    s.update(TA=vm(10, 24, 128), TB=vm(10, 24, 128), DA=vm(10, 48, 128), DB=vm(10, 32, 128))
    s.update(C3=vm(10, 48, 128), T3=vm(8, 32, 128), KA=vm(10, 48, 128), KB=vm(10, 48, 128), ST3=vm(8, 32, 128))
    s.update(WX3=vm(9, 32, 128), WY3=vm(8, 40, 128))
    for name in ("WXM3", "WXP3", "WYM3", "WYP3", "WZM3", "WZP3", "D3", "SD3"):
        s[name] = vm(8, 32, 128)
    s.update(G3=vm(10, 8, 4, 128), R3=vm(8, 16, 128), T32=vm(8, 16, 128), D32=vm(8, 24, 128))
    return s


def kernel(k_ref, g_ref, c_ref, v_ref, o_ref, s):
    gx, gy, gz = (lax.axis_index(a) for a in ("gx", "gy", "gz"))
    one = lambda cond: jnp.where(cond, F32(1.0), F32(0.0))
    mx = {-1: one(gx > 0), 0: F32(1.0), 1: one(gx < NX - 1)}
    my = {-1: one(gy > 0), 0: F32(1.0), 1: one(gy < NY - 1)}
    mz = {-1: one(gz > 0), 0: F32(1.0), 1: one(gz < NZ - 1)}
    started = []

    def target(o):
        return (lax.rem(gx + o[0] + NX, NX), lax.rem(gy + o[1] + NY, NY), lax.rem(gz + o[2] + NZ, NZ))

    def send(src, dst, ss, rs, o):
        copy = pltpu.make_async_remote_copy(
            src_ref=src, dst_ref=dst, send_sem=ss, recv_sem=rs, device_id=target(o), device_id_type=MESH
        )
        copy.start()
        started.append(copy)
        return copy

    def arrive(copies):
        for copy in copies:
            copy.wait_recv()

    barrier = pltpu.get_barrier_semaphore()
    for o in SIX:
        pl.semaphore_signal(barrier, inc=1, device_id=target(o), device_id_type=MESH)

    def pack_fine(plane, k, p, acc):
        s["YB"][k, 0, p] = plane[0:1]
        s["YB"][k, 1, p] = plane[31:32]
        at = lane((32, 128))
        mine = (at == (2 * p) % 128) | (at == (2 * p - 1) % 128)
        moved = roll(plane, 2 * p)
        return jnp.where(mine, moved, acc)

    def send_fine(low, high, k):
        out = []
        ss, rs = s["ss0"], s["rs0"]
        yb, rx, ry, rz = s["YB"], s["RX"], s["RY"], s["RZ"]
        out.append(send(yb.at[k, 1], ry.at[k, 0], ss.at[k, 0], rs.at[k, 0], (0, 1, 0)))
        out.append(send(yb.at[k, 0], ry.at[k, 1], ss.at[k, 1], rs.at[k, 1], (0, -1, 0)))
        out.append(send(high, rx.at[k, 0], ss.at[k, 2], rs.at[k, 2], (1, 0, 0)))
        out.append(send(low, rx.at[k, 1], ss.at[k, 3], rs.at[k, 3], (-1, 0, 0)))
        out.append(send(s["PZ"].at[k], rz.at[k, 0], ss.at[k, 4], rs.at[k, 4], (0, 0, 1)))
        out.append(send(s["PZ"].at[k], rz.at[k, 1], ss.at[k, 5], rs.at[k, 5], (0, 0, -1)))
        return out

    def take_fine(v, k, copies):
        arrive(copies)
        v[0, 8:40, :] = s["RX"][k, 0] * mx[-1]
        v[17, 8:40, :] = s["RX"][k, 1] * mx[1]
        v[1:17, 7:8, :] = s["RY"][k, 0] * my[-1]
        v[1:17, 40:41, :] = s["RY"][k, 1] * my[1]
        odd = lane((32, 128)) % 2 == 1
        s["MZ"][k] = jnp.where(odd, roll(s["RZ"][k, 1], -1) * mz[1], roll(s["RZ"][k, 0], 1) * mz[-1])

    def fine_z(k, extra=None):
        def get(p, v):
            at = lane((32, 128))
            edge = roll(s["MZ"][k], -2 * p)
            if extra is not None:
                edge = edge + extra(p)
            return jnp.where(at == 0, edge, roll(v, 1)), jnp.where(at == 127, edge, roll(v, -1))

        return get

    def plain_z(p, v):
        return roll(v, 1), roll(v, -1)

    def closed_z(p, v):
        at = lane(v.shape)
        return jnp.where(at == 0, 0.0, roll(v, 1)), jnp.where(at == 127, 0.0, roll(v, -1))

    def weights(l, n, rows, scale, zs):
        c, wx, wy = s["C" + l], s["WX" + l], s["WY" + l]
        h = F32(0.5 * scale)
        for p in range(n + 1):
            wx[p] = h * (c[p, 8 : 8 + rows, :] + c[p + 1, 8 : 8 + rows, :])
        for p in range(n):
            wy[p] = h * (c[p + 1, 8 : 16 + rows, :] + c[p + 1, 7 : 15 + rows, :])
            mid = c[p + 1, 8 : 8 + rows, :]
            zm, zp = zs(p, mid)
            wzm, wzp = h * (mid + zm), h * (mid + zp)
            d = wx[p] + wx[p + 1] + wy[p, 0:rows] + wy[p, 1 : rows + 1] + wzm + wzp
            s["WZM" + l][p], s["WZP" + l][p], s["D" + l][p] = wzm, wzp, d
            s["SD" + l][p] = jnp.where(mid > 0, F32(OMEGA) / d, 0.0)

    def gathered(l, v, p, rows, right, zs):
        wx, wy = s["WX" + l], s["WY" + l]
        mid = v[p + 1, 8 : 8 + rows, :]
        zm, zp = zs(p, mid)
        total = right + wx[p] * v[p, 8 : 8 + rows, :] + wx[p + 1] * v[p + 2, 8 : 8 + rows, :]
        total = total + wy[p, 0:rows] * v[p + 1, 7 : 7 + rows, :]
        total = total + wy[p, 1 : rows + 1] * v[p + 1, 9 : 9 + rows, :]
        total = total + s["WZM" + l][p] * zm + s["WZP" + l][p] * zp
        return mid, total

    def swept(l, v, p, rows, right, zs):
        mid, total = gathered(l, v, p, rows, right, zs)
        return mid * F32(1.0 - OMEGA) + s["SD" + l][p] * total

    def residual(l, v, p, rows, right, zs):
        mid, total = gathered(l, v, p, rows, right, zs)
        return total - s["D" + l][p] * mid

    to_one = picks(lambda r, c: r // 2 + 32 == c, value=0.125)
    to_two = [
        picks(lambda r, c, p=p: (c // 32 == p) & (r // 2 == c % 32 + 16), value=0.125) for p in range(4)
    ]
    to_three = [
        picks(lambda r, c, q=q: (c // 16 == q) & (r // 2 == c % 16 + 16) & (c < 64), value=0.125)
        for q in range(4)
    ]

    def restrict_fine(plane, k):
        rs = s["RS0"]
        for q in range(8):
            rs[q] = plane(2 * q) + plane(2 * q + 1)
        half = rs[:, pl.ds(0, 16, stride=2), :] + rs[:, pl.ds(1, 16, stride=2), :]
        block = mm(half.reshape(128, 128), to_one).reshape(8, 16, 128)
        s["B1" + k][...] = block
        at = lane((16, 128))
        acc = jnp.zeros((16, 128), F32)
        for p in range(8):
            acc = jnp.where((at >= 16 * p) & (at < 16 * p + 8), roll(block[p], 16 * p - 32), acc)
            acc = jnp.where((at >= 16 * p + 8) & (at < 16 * p + 16), roll(block[p], 16 * p + 8 - 88), acc)
        s["PZ1" + k][...] = acc

    def restrict_one(plane, first, k):
        rs = s["RS1"]
        rows = 24 if first == 4 else 16
        for q in range(4):
            rs[q, 0:rows] = plane(2 * q) + plane(2 * q + 1)
        half = rs[:, pl.ds(first, 8, stride=2), :] + rs[:, pl.ds(first + 1, 8, stride=2), :]
        s["PB2" + k][...] = sum(mm(half[p], to_two[p]) for p in range(4))

    def restrict_two(plane, k):
        rs, qs = s["RS2"], s["QS"]
        for q in range(8):
            rs[q] = plane(2 * q) + plane(2 * q + 1)
        half = rs[:, pl.ds(0, 4, stride=2), :] + rs[:, pl.ds(1, 4, stride=2), :]
        for q in range(4):
            qs[q, 0:4] = half[2 * q]
            qs[q, 4:8] = half[2 * q + 1]
        s["PB3" + k][...] = sum(mm(qs[q], to_three[q]) for q in range(4))

    def send_one(k, h):
        out = []
        b, pz = s["B1" + k], s["PZ1" + k]
        for i, (dx, dy, dz) in enumerate(AROUND):
            if dz:
                src, dst = pz, s["RZ1" + k].at[side(-dz), 1 - dx, 1 - dy]
            else:
                xs = pl.ds(8 - h, h) if dx > 0 else pl.ds(0, h)
                ys = pl.ds(8, 8) if dy > 0 else pl.ds(0, 8)
                if dx and dy:
                    src, dst = b.at[xs, ys], s["RE1" + k].at[side(-dx), side(-dy)]
                elif dx:
                    src, dst = b.at[xs], s["RX1" + k].at[side(-dx)]
                else:
                    src, dst = b.at[:, ys], s["RY1" + k].at[side(-dy)]
            out.append(send(src, dst, s["ss1" + k].at[i], s["rs1" + k].at[i], (dx, dy, dz)))
        return out

    def take_one(e, k, h, copies):
        arrive(copies)
        b, rx, ry, re, rz, zs = (s[n + k] for n in ("B1", "RX1", "RY1", "RE1", "RZ1", "ZS"))
        first = lane((16, 128)) % 16 >= 8

        def beside(dx, dy):
            left = rz[0, 1 + dx, 1 + dy] * mz[-1]
            right = roll(rz[1, 1 + dx, 1 + dy], 80) * mz[1]
            return jnp.where(first, left, right) * (mx[dx] * my[dy])

        for dx in (-1, 0, 1):
            zs[1 + dx, 12:28] = beside(dx, 0)
            zs[1 + dx, 12 - h : 12] = beside(dx, -1)[16 - h : 16]
            zs[1 + dx, 28 : 28 + h] = beside(dx, 1)[0:h]
            count, base, start = (8, 5, 0) if dx == 0 else ((h, 5 - h, 8 - h) if dx < 0 else (h, 13, 0))
            planes = pl.ds(base, count)
            if dx == 0:
                e[planes, 12:28, :] = b[...]
                e[planes, 12 - h : 12, :] = ry[0, :, 8 - h : 8, :] * my[-1]
                e[planes, 28 : 28 + h, :] = ry[1, :, 0:h, :] * my[1]
            else:
                e[planes, 12:28, :] = rx[side(dx)] * mx[dx]
                e[planes, 12 - h : 12, :] = re[side(dx), 0, :, 8 - h : 8, :] * (mx[dx] * my[-1])
                e[planes, 28 : 28 + h, :] = re[side(dx), 1, :, 0:h, :] * (mx[dx] * my[1])
            lo, hi = (8, 32) if h == 4 else (0, 40)
            at = lane((hi - lo, 128))
            halo = ((at >= 24) & (at < 32)) | ((at >= 96) & (at < 104))
            for i in range(count):
                moved = roll(zs[1 + dx, lo:hi], 16 - 16 * (start + i))
                e[base + i, lo:hi, :] = jnp.where(halo, moved, e[base + i, lo:hi, :])

    def send_two(k):
        out = []
        for i, (a, dy, dz) in enumerate(WIDE):
            dst = s["S2" + k].at[gx, 1 - dy, 1 - dz]
            out.append(send(s["PB2" + k], dst, s["ss2" + k].at[i], s["rs2" + k].at[i], (a, dy, dz)))
        s["S2" + k][gx, 1, 1] = s["PB2" + k][...]
        return out

    def take_two(e, k, copies):
        arrive(copies)
        at = lane((8, 128)) // 32
        for x in range(NX):
            for dy in (-1, 0, 1):
                blocks = [s["S2" + k][x, 1 + dy, 1 + dz] * (my[dy] * mz[dz]) for dz in (-1, 0, 1)]
                for p in range(4):
                    val = jnp.zeros((8, 128), F32)
                    for z in range(3):
                        val = jnp.where(at == z, roll(blocks[z], 32 * (z - p)), val)
                    e[1 + 4 * x + p, 16 + 8 * dy : 24 + 8 * dy, :] = val

    def send_z(k):
        out = []
        for a in range(1, NZ):
            dst = s["S3" + k].at[gz]
            out.append(send(s["PB3" + k], dst, s["ss3" + k].at[a], s["rs3" + k].at[a], (0, 0, a)))
        s["S3" + k][gz] = s["PB3" + k][...]
        return out

    def pass_y(k, copies):
        arrive(copies)
        at = lane((8, 128)) // 16
        for q in range(4):
            val = jnp.zeros((8, 128), F32)
            for j in range(NZ):
                val = jnp.where(at == j, roll(s["S3" + k][j], 16 * (j - q)), val)
            s["YS" + k][2 * q] = val[0:4]
            s["YS" + k][2 * q + 1] = val[4:8]
        out = []
        for a in range(1, NY):
            dst = s["S4" + k].at[gy]
            out.append(send(s["YS" + k], dst, s["ss4" + k].at[a], s["rs4" + k].at[a], (0, a, 0)))
        s["S4" + k][gy] = s["YS" + k][...]
        return out

    for name in ("C1", "G1", "EA1", "EB1", "C2", "G2", "EA2", "EB2"):
        s[name][...] = jnp.zeros((18, 40, 128), F32)
    for name in ("C3", "KA", "KB"):
        s[name][...] = jnp.zeros((10, 48, 128), F32)
    s["ZSc"][...] = jnp.zeros((3, 40, 128), F32)
    s["U2"][...] = jnp.zeros((20, 24, 128), F32)
    s["R3"][...] = jnp.zeros((8, 16, 128), F32)
    s["G3"][...] = jnp.zeros((10, 8, 4, 128), F32)
    for k, ref, v in ((0, c_ref, "C0"), (1, v_ref, "V0")):
        acc = jnp.zeros((32, 128), F32)
        for p in range(16):
            plane = ref[p]
            s[v][p + 1, 8:40, :] = plane
            acc = pack_fine(plane, k, p, acc)
        s["PZ"][k] = acc
    pl.semaphore_wait(barrier, len(SIX))

    cc = send_fine(c_ref.at[0], c_ref.at[15], 0)
    vv = send_fine(v_ref.at[0], v_ref.at[15], 1)
    restrict_fine(lambda p: c_ref[p], "c")
    restrict_one(lambda p: s["B1c"][p], 0, "c")
    take_fine(s["C0"], 0, cc)
    weights("0", 16, 32, 1.0, fine_z(0))
    take_fine(s["V0"], 1, vv)

    def sweep_fine(src, dst, zs, k):
        acc = jnp.zeros((32, 128), F32)
        for p in range(16):
            new = swept("0", s[src], p, 32, g_ref[p], zs)
            s[dst][p + 1, 8:40, :] = new
            acc = pack_fine(new, k, p, acc)
        s["PZ"][k] = acc
        return send_fine(s[dst].at[1, 8:40], s[dst].at[16, 8:40], k)

    copies = sweep_fine("V0", "V1", fine_z(1), 2)
    take_fine(s["V1"], 2, copies)
    copies = sweep_fine("V1", "X0", fine_z(2), 3)
    c_one = send_one("c", 5)
    take_fine(s["X0"], 3, copies)
    restrict_fine(lambda p: residual("0", s["X0"], p, 32, g_ref[p], fine_z(3)), "g")

    g_one = send_one("g", 4)
    take_one(s["C1"], "c", 5, c_one)
    c_two = send_two("c")
    weights("1", 16, 24, 0.25, plain_z)
    take_one(s["G1"], "g", 4, g_one)

    def begin(l):
        for p in range(16):
            s["EA" + l][p + 1, 8:32, :] = s["SD" + l][p] * s["G" + l][p + 1, 8:32, :]

    def sweep(l, src, dst):
        for p in range(16):
            right = s["G" + l][p + 1, 8:32, :]
            s[dst][p + 1, 8:32, :] = swept(l, s[src], p, 24, right, plain_z)

    def left(l, src):
        return lambda p: residual(l, s[src], p, 24, s["G" + l][p + 1, 8:32, :], plain_z)

    begin("1")
    sweep("1", "EA1", "EB1")
    rest = left("1", "EB1")
    restrict_one(lambda p: rest(p + 4), 4, "g")

    g_two = send_two("g")
    take_two(s["C2"], "c", c_two)
    restrict_two(lambda p: s["C2"][p + 1, 16:24, :], "c")
    c_z = send_z("c")
    weights("2", 16, 24, 0.0625, plain_z)
    take_two(s["G2"], "g", g_two)
    begin("2")
    sweep("2", "EA2", "EB2")
    rest2 = left("2", "EB2")
    restrict_two(lambda p: rest2(p)[8:16], "g")

    g_z = send_z("g")
    c_y = pass_y("c", c_z)
    g_y = pass_y("g", g_z)
    arrive(c_y)
    for g in range(NY):
        s["C3"][1:9, 8 + 4 * g : 12 + 4 * g, :] = s["S4c"][g]
    weights("3", 8, 32, 0.015625, closed_z)
    at = lane((32, 128))
    for p in range(8):
        inv = F32(1.0) / s["D3"][p]
        s["SD3"][p] = inv
        s["WXM3"][p] = s["WX3"][p] * inv
        s["WXP3"][p] = s["WX3"][p + 1] * inv
        s["WYM3"][p] = s["WY3"][p, 0:32] * inv
        s["WYP3"][p] = s["WY3"][p, 1:33] * inv
        s["WZM3"][p] = jnp.where(at == 0, 0.0, s["WZM3"][p] * inv)
        s["WZP3"][p] = jnp.where(at == 127, 0.0, s["WZP3"][p] * inv)
    arrive(g_y)
    for g in range(NY):
        s["T3"][:, 4 * g : 4 * g + 4, :] = s["S4g"][g]
    theta = constants()[1]
    for p in range(8):
        t = s["T3"][p] * s["SD3"][p]
        s["T3"][p] = t
        d = t * F32(1.0 / theta)
        s["ST3"][p] = d
        s["KA"][p + 1, 8:40, :] = d

    def cheb(src, dst, i):
        a, b = k_ref[2 * i], k_ref[2 * i + 1]
        v = s[src]
        for p in range(8):
            e = v[p + 1, 8:40, :]
            r = s["T3"][p] - e + s["WXM3"][p] * v[p, 8:40, :] + s["WXP3"][p] * v[p + 2, 8:40, :]
            r = r + s["WYM3"][p] * v[p + 1, 7:39, :] + s["WYP3"][p] * v[p + 1, 9:41, :]
            r = r + s["WZM3"][p] * roll(e, 1) + s["WZP3"][p] * roll(e, -1)
            d = a * s["ST3"][p] + b * r
            s["ST3"][p] = d
            s[dst][p + 1, 8:40, :] = e + d

    def two(i, carry):
        cheb("KA", "KB", 2 * i)
        cheb("KB", "KA", 2 * i + 1)
        return carry

    lax.fori_loop(0, (CHEB - 1) // 2, two, 0)
    cheb("KA", "KB", CHEB - 2)

    for g in range(NY):
        s["G3"][g + 1] = s["KB"][1:9, 8 + 4 * g : 12 + 4 * g, :]
    for j in range(3):
        s["R3"][:, 4 * j : 4 * j + 4, :] = s["G3"][gy + j]
    from_three = picks(lambda r, c: (r == 16 * gz - 16 + c // 2) & (c < 96))
    s["T32"][...] = mm(s["R3"][...].reshape(128, 128), from_three).reshape(8, 16, 128)
    for o in (0, 1):
        s["D32"][:, pl.ds(o, 12, stride=2), :] = s["T32"][:, 0:12, :]
    for p in range(16):
        s["EA2"][p + 1, 8:32, :] = s["EB2"][p + 1, 8:32, :] + s["D32"][p // 2]
    sweep("2", "EA2", "EB2")
    for p in range(16):
        right = s["G2"][p + 1, 8:32, :]
        s["U2"][p + 2] = swept("2", s["EB2"], p, 24, right, plain_z)

    from_two = picks(lambda r, c: (r == 16 + c // 2) & (c >= 24) & (c < 104))
    part = s["U2"][pl.ds(4 * gx, 8)]
    s["T21"][...] = mm(part.reshape(192, 128), from_two).reshape(8, 24, 128)
    for o in (0, 1):
        s["D21"][:, pl.ds(o, 12, stride=2), :] = s["T21"][:, 6:18, :]
    for p in range(16):
        s["EA1"][p + 1, 8:32, :] = s["EB1"][p + 1, 8:32, :] + s["D21"][p // 2]
    sweep("1", "EA1", "EB1")
    sweep("1", "EB1", "EA1")

    from_one = picks(
        lambda r, c: ((c < 128) & (r == 32 + c // 2)) | ((c == 128) & (r == 31)) | ((c == 255) & (r == 96)), 256
    )
    wide = mm(s["EA1"][4:14, 8:32, :].reshape(240, 128), from_one)
    s["TA"][...] = wide[:, 0:128].reshape(10, 24, 128)
    s["TB"][...] = wide[:, 128:256].reshape(10, 24, 128)
    for o in (0, 1):
        s["DA"][:, pl.ds(8 + o, 16, stride=2), :] = s["TA"][:, 4:20, :]
        s["DB"][:, pl.ds(o, 16, stride=2), :] = s["TB"][:, 4:20, :]
    for i in range(18):
        j = (i + 1) // 2
        s["VP"][i, 8:40, :] = s["X0"][i, 8:40, :] + s["DA"][j, 8:40, :]
        if 0 < i < 17:
            s["VP"][i, 7:8, :] = s["X0"][i, 7:8, :] + s["TA"][j, 3:4, :]
            s["VP"][i, 40:41, :] = s["X0"][i, 40:41, :] + s["TA"][j, 20:21, :]
    copies = sweep_fine("VP", "VQ", fine_z(3, lambda p: s["DB"][(p + 2) // 2]), 4)
    take_fine(s["VQ"], 4, copies)
    for p in range(16):
        o_ref[p] = swept("0", s["VQ"], p, 32, g_ref[p], fine_z(4))
    for copy in started:
        copy.wait_send()


def on_device(right_side, coefficient, guess):
    table = jnp.asarray(constants()[0])
    vmem = pl.BlockSpec(memory_space=pltpu.VMEM)
    return pl.pallas_call(
        kernel,
        out_shape=jax.ShapeDtypeStruct((16, 32, 128), F32),
        in_specs=[pl.BlockSpec(memory_space=pltpu.SMEM), vmem, vmem, vmem],
        out_specs=vmem,
        scratch_shapes=[build_scratch()],
        compiler_params=pltpu.CompilerParams(
            collective_id=0, has_side_effects=True, vmem_limit_bytes=56 * 2**20
        ),
    )(table, right_side, coefficient, guess)


def solution(mesh):
    spec = P("gx", "gy", "gz")
    return jax.shard_map(on_device, mesh=mesh, in_specs=(spec, spec, spec), out_specs=spec, check_vma=False)
```

```python
import itertools

import jax
import jax.numpy as jnp
import numpy as np
from jax import lax
from jax.experimental import pallas as pl
from jax.experimental.pallas import tpu as pltpu
from jax.sharding import PartitionSpec as P

CHEB = 20
OMEGA = 2.0 / 3.0
CHEB_LOW = 0.1
CHEB_HIGH = 2.0
MESH = pl.DeviceIdType.MESH
F32 = jnp.float32
NX, NY, NZ = 4, 8, 8
SIX = ((1, 0, 0), (-1, 0, 0), (0, 1, 0), (0, -1, 0), (0, 0, 1), (0, 0, -1))
AROUND = sorted(
    (o for o in itertools.product((-1, 0, 1), repeat=3) if o != (0, 0, 0)),
    key=lambda o: -(abs(o[0]) + abs(o[1]) + abs(o[2])),
)
WIDE = sorted(
    (o for o in itertools.product(range(NX), (-1, 0, 1), (-1, 0, 1)) if o != (0, 0, 0)),
    key=lambda o: -((o[0] != 0) + (o[0] == 2) + abs(o[1]) + abs(o[2])),
)
CHIPS = sorted(
    (o for o in itertools.product((0,), range(NY), range(0, NZ, 2)) if o != (0, 0, 0)),
    key=lambda o: -(min(o[1], NY - o[1]) + min(o[2], NZ - o[2]) // 2),
)
NEAR = {(o[0], o[1] % NY, o[2] % NZ) for o in SIX}
FAR = [o for o in CHIPS if o not in NEAR]


def side(d):
    return 0 if d < 0 else 1


def constants():
    theta, delta = 0.5 * (CHEB_HIGH + CHEB_LOW), 0.5 * (CHEB_HIGH - CHEB_LOW)
    sigma = theta / delta
    rho, out = np.float32(1.0 / sigma), []
    for _ in range(CHEB - 1):
        rho_next = np.float32(1.0 / (2.0 * sigma - rho))
        out += [np.float32(rho_next * rho), np.float32(2.0 * rho_next / delta)]
        rho = rho_next
    return np.array(out, np.float32), theta


def lane(shape):
    return lax.broadcasted_iota(jnp.int32, shape, len(shape) - 1)


def roll(x, by):
    return pltpu.roll(x, by % 128, x.ndim - 1)


def mm(x, m):
    return lax.dot_general(
        x, m, (((1,), (0,)), ((), ())), precision=lax.Precision.HIGHEST, preferred_element_type=F32
    )


def picks(condition, width=128, value=1.0):
    row = lax.broadcasted_iota(jnp.int32, (128, width), 0)
    col = lax.broadcasted_iota(jnp.int32, (128, width), 1)
    return jnp.where(condition(row, col), F32(value), F32(0.0))


def vm(*shape):
    return pltpu.VMEM(shape, F32)


def dma(*shape):
    return pltpu.SemaphoreType.DMA(shape)


def build_scratch():
    s = {}
    for name in ("C0", "V0", "V1", "X0", "VP", "VQ"):
        s[name] = vm(18, 48, 128)
    s.update(WX0=vm(17, 32, 128), WY0=vm(16, 40, 128))
    for name in ("WZM0", "WZP0", "D0", "SD0"):
        s[name] = vm(16, 32, 128)
    s.update(
        YB=vm(2, 5, 16, 1, 128), PZ=vm(5, 32, 128),
        RX=vm(5, 2, 32, 128), RY=vm(2, 5, 16, 1, 128), RZ=vm(2, 5, 32, 128), MZ=vm(5, 32, 128),
        ss0=dma(5, 6), rs0=dma(5, 6), hs=dma(8), GV=vm(16, 32, 128), OV=vm(16, 32, 128),
    )
    s.update(RS0=vm(8, 32, 128), RS1=vm(4, 24, 128), RS2=vm(8, 8, 128), QS=vm(4, 8, 128))
    for k, h in (("c", 5), ("g", 4)):
        s["B1" + k] = vm(8, 16, 128)
        s["PZ1" + k] = vm(16, 128)
        s["RX1" + k] = vm(2, h, 16, 128)
        s["RY1" + k] = vm(2, 8, 8, 128)
        s["RE1" + k] = vm(2, 2, h, 8, 128)
        s["RZ1" + k] = vm(2, 3, 3, 16, 128)
        s["ss1" + k], s["rs1" + k] = dma(26), dma(26)
        s["ZS" + k] = vm(3, 40, 128)
        s["PB2" + k] = vm(8, 128)
        s["S2" + k] = vm(NX, 3, 3, 8, 128)
        s["ss2" + k], s["rs2" + k] = dma(len(WIDE)), dma(len(WIDE))
        s["PB3" + k] = vm(8, 128)
        s["S3" + k] = vm(8, 128)
        s["YS" + k] = vm(8, 128)
        s["S4" + k] = vm(NY, NZ // 2, 8, 128)
        s["ss3" + k], s["rs3" + k] = dma(1), dma(1)
        s["ss4" + k], s["rs4" + k] = dma(len(CHIPS)), dma(len(CHIPS))
    for l in ("1", "2"):
        for name in ("C", "G", "EA", "EB"):
            s[name + l] = vm(18, 40, 128)
        s.update({"WX" + l: vm(17, 24, 128), "WY" + l: vm(16, 32, 128)})
        for name in ("WZM", "WZP", "D", "SD"):
            s[name + l] = vm(16, 24, 128)
    s["K"] = pltpu.SMEM((2 * (CHEB - 1),), F32)
    s.update(U2=vm(20, 24, 128), T21=vm(8, 24, 128), D21=vm(8, 24, 128))
    s.update(TA=vm(10, 24, 128), TB=vm(10, 24, 128), DA=vm(10, 48, 128), DB=vm(10, 32, 128))
    s.update(C3=vm(10, 48, 128), T3=vm(8, 32, 128), KA=vm(10, 48, 128), KB=vm(10, 48, 128), ST3=vm(8, 32, 128))
    s.update(WX3=vm(9, 32, 128), WY3=vm(8, 40, 128))
    for name in ("WXM3", "WXP3", "WYM3", "WYP3", "WZM3", "WZP3", "D3", "SD3"):
        s[name] = vm(8, 32, 128)
    s.update(G3=vm(10, 8, 4, 128), R3=vm(8, 16, 128), T32=vm(8, 16, 128), D32=vm(8, 24, 128))
    return s


def kernel(g_hbm, c_hbm, v_hbm, o_ref, s):
    gx, gy, gz = (lax.axis_index(a) for a in ("gx", "gy", "gz"))
    here = {
        0: {-1: gx > 0, 1: gx < NX - 1},
        1: {-1: gy > 0, 1: gy < NY - 1},
        2: {-1: gz > 0, 1: gz < NZ - 1},
    }
    core = lax.rem(gz, 2)
    started = []

    def exists(o, axes=(0, 1, 2)):
        cond = None
        for axis in axes:
            if o[axis]:
                cond = here[axis][o[axis]] if cond is None else cond & here[axis][o[axis]]
        return cond

    def keep(x, *o, axes=(0, 1, 2)):
        cond = exists(o, axes)
        return x if cond is None else jnp.where(cond, x, 0.0)

    def when(cond, act):
        if cond is None:
            act()
        else:
            pl.when(cond)(act)

    def target(o):
        return (lax.rem(gx + o[0] + NX, NX), lax.rem(gy + o[1] + NY, NY), lax.rem(gz + o[2] + NZ, NZ))

    def send(src, dst, ss, rs, o, axes=(0, 1, 2), to=None):
        copy = pltpu.make_async_remote_copy(
            src_ref=src, dst_ref=dst, send_sem=ss, recv_sem=rs,
            device_id=target(o) if to is None else to, device_id_type=MESH,
        )
        out = exists(o, axes)
        when(out, copy.start)
        started.append((copy, out))
        return copy, exists(tuple(-d for d in o), axes)

    def arrive(copies):
        for copy, cond in copies:
            when(cond, copy.wait_recv)

    barrier = pltpu.get_barrier_semaphore()
    for o in SIX:
        pl.semaphore_signal(barrier, inc=1, device_id=target(o), device_id_type=MESH)
    main = (pl.ds(1, 16), pl.ds(8, 32))
    loads = [
        pltpu.make_async_copy(c_hbm, s["C0"].at[main], s["hs"].at[0]),
        pltpu.make_async_copy(v_hbm, s["V0"].at[main], s["hs"].at[1]),
        pltpu.make_async_copy(g_hbm, s["GV"], s["hs"].at[2]),
    ]
    for load in loads:
        load.start()
    for o in FAR:
        pl.semaphore_signal(barrier, inc=1, device_id=target(o), device_id_type=MESH)

    def pack_fine(plane, k, p, acc):
        s["YB"][0, k, p] = plane[0:1]
        s["YB"][1, k, p] = plane[31:32]
        at = lane((32, 128))
        mine = (at == (2 * p) % 128) | (at == (2 * p - 1) % 128)
        return jnp.where(mine, roll(plane, 2 * p), acc)

    def send_fine(names, k):
        out = []
        ss, rs = s["ss0"], s["rs0"]
        yb, rx, ry, rz, pz = s["YB"], s["RX"], s["RY"], s["RZ"], s["PZ"]
        ks = pl.ds(k, len(names))
        out.append(send(yb.at[1, ks], ry.at[0, ks], ss.at[k, 0], rs.at[k, 0], (0, 1, 0)))
        out.append(send(yb.at[0, ks], ry.at[1, ks], ss.at[k, 1], rs.at[k, 1], (0, -1, 0)))
        for i, name in enumerate(names):
            low, high = s[name].at[1, pl.ds(8, 32)], s[name].at[16, pl.ds(8, 32)]
            out.append(send(high, rx.at[k + i, 0], ss.at[k + i, 2], rs.at[k + i, 2], (1, 0, 0)))
            out.append(send(low, rx.at[k + i, 1], ss.at[k + i, 3], rs.at[k + i, 3], (-1, 0, 0)))
        out.append(send(pz.at[ks], rz.at[0, ks], ss.at[k, 4], rs.at[k, 4], (0, 0, 1)))
        out.append(send(pz.at[ks], rz.at[1, ks], ss.at[k, 5], rs.at[k, 5], (0, 0, -1)))
        return out

    def take_fine(name, k):
        v = s[name]
        v[0, 8:40, :] = keep(s["RX"][k, 0], -1, 0, 0)
        v[17, 8:40, :] = keep(s["RX"][k, 1], 1, 0, 0)
        v[1:17, 7:8, :] = keep(s["RY"][0, k], 0, -1, 0)
        v[1:17, 40:41, :] = keep(s["RY"][1, k], 0, 1, 0)
        odd = lane((32, 128)) % 2 == 1
        right, left = keep(s["RZ"][1, k], 0, 0, 1), keep(s["RZ"][0, k], 0, 0, -1)
        s["MZ"][k] = jnp.where(odd, roll(right, -1), roll(left, 1))

    def fine_z(k, extra=None):
        def get(p, v):
            at = lane((32, 128))
            edge = roll(s["MZ"][k], -2 * p)
            if extra is not None:
                edge = edge + extra(p)
            return jnp.where(at == 0, edge, roll(v, 1)), jnp.where(at == 127, edge, roll(v, -1))

        return get

    def plain_z(p, v):
        return roll(v, 1), roll(v, -1)

    def closed_z(p, v):
        at = lane(v.shape)
        return jnp.where(at == 0, 0.0, roll(v, 1)), jnp.where(at == 127, 0.0, roll(v, -1))

    def weights(l, n, rows, scale, zs):
        c, wx, wy = s["C" + l], s["WX" + l], s["WY" + l]
        h = F32(0.5 * scale)
        for p in range(n + 1):
            wx[p] = h * (c[p, 8 : 8 + rows, :] + c[p + 1, 8 : 8 + rows, :])
        for p in range(n):
            wy[p] = h * (c[p + 1, 8 : 16 + rows, :] + c[p + 1, 7 : 15 + rows, :])
            mid = c[p + 1, 8 : 8 + rows, :]
            zm, zp = zs(p, mid)
            wzm, wzp = h * (mid + zm), h * (mid + zp)
            d = wx[p] + wx[p + 1] + wy[p, 0:rows] + wy[p, 1 : rows + 1] + wzm + wzp
            s["WZM" + l][p], s["WZP" + l][p], s["D" + l][p] = wzm, wzp, d
            s["SD" + l][p] = jnp.where(mid > 0, F32(OMEGA) / d, 0.0)

    def gathered(l, v, p, rows, right, zs):
        wx, wy = s["WX" + l], s["WY" + l]
        mid = v[p + 1, 8 : 8 + rows, :]
        zm, zp = zs(p, mid)
        total = right + wx[p] * v[p, 8 : 8 + rows, :] + wx[p + 1] * v[p + 2, 8 : 8 + rows, :]
        total = total + wy[p, 0:rows] * v[p + 1, 7 : 7 + rows, :]
        total = total + wy[p, 1 : rows + 1] * v[p + 1, 9 : 9 + rows, :]
        total = total + s["WZM" + l][p] * zm + s["WZP" + l][p] * zp
        return mid, total

    def swept(l, v, p, rows, right, zs):
        mid, total = gathered(l, v, p, rows, right, zs)
        return mid * F32(1.0 - OMEGA) + s["SD" + l][p] * total

    def residual(l, v, p, rows, right, zs):
        mid, total = gathered(l, v, p, rows, right, zs)
        return total - s["D" + l][p] * mid

    to_one = picks(lambda r, c: r // 2 + 32 == c, value=0.125)
    to_two = [
        picks(lambda r, c, p=p: (c // 32 == p) & (r // 2 == c % 32 + 16), value=0.125) for p in range(4)
    ]
    to_three = [
        picks(lambda r, c, q=q: (c // 16 == 2 * q + core) & (r // 2 == c % 16 + 16), value=0.125)
        for q in range(4)
    ]

    def restrict_fine(plane, k):
        rs = s["RS0"]
        for q in range(8):
            rs[q] = plane(2 * q) + plane(2 * q + 1)
        half = rs[:, pl.ds(0, 16, stride=2), :] + rs[:, pl.ds(1, 16, stride=2), :]
        block = mm(half.reshape(128, 128), to_one).reshape(8, 16, 128)
        s["B1" + k][...] = block
        at = lane((16, 128))
        acc = jnp.zeros((16, 128), F32)
        for p in range(8):
            acc = jnp.where((at >= 16 * p) & (at < 16 * p + 8), roll(block[p], 16 * p - 32), acc)
            acc = jnp.where((at >= 16 * p + 8) & (at < 16 * p + 16), roll(block[p], 16 * p + 8 - 88), acc)
        s["PZ1" + k][...] = acc

    def restrict_one(plane, first, k):
        rs = s["RS1"]
        rows = 24 if first == 4 else 16
        for q in range(4):
            rs[q, 0:rows] = plane(2 * q) + plane(2 * q + 1)
        half = rs[:, pl.ds(first, 8, stride=2), :] + rs[:, pl.ds(first + 1, 8, stride=2), :]
        s["PB2" + k][...] = sum(mm(half[p], to_two[p]) for p in range(4))

    def restrict_two(plane, k):
        rs, qs = s["RS2"], s["QS"]
        for q in range(8):
            rs[q] = plane(2 * q) + plane(2 * q + 1)
        half = rs[:, pl.ds(0, 4, stride=2), :] + rs[:, pl.ds(1, 4, stride=2), :]
        for q in range(4):
            qs[q, 0:4] = half[2 * q]
            qs[q, 4:8] = half[2 * q + 1]
        s["PB3" + k][...] = sum(mm(qs[q], to_three[q]) for q in range(4))

    def send_one(k, h):
        out = []
        b, pz = s["B1" + k], s["PZ1" + k]
        for i, (dx, dy, dz) in enumerate(AROUND):
            if dz:
                src, dst = pz, s["RZ1" + k].at[side(-dz), 1 - dx, 1 - dy]
            else:
                xs = pl.ds(8 - h, h) if dx > 0 else pl.ds(0, h)
                ys = pl.ds(8, 8) if dy > 0 else pl.ds(0, 8)
                if dx and dy:
                    src, dst = b.at[xs, ys], s["RE1" + k].at[side(-dx), side(-dy)]
                elif dx:
                    src, dst = b.at[xs], s["RX1" + k].at[side(-dx)]
                else:
                    src, dst = b.at[:, ys], s["RY1" + k].at[side(-dy)]
            out.append(send(src, dst, s["ss1" + k].at[i], s["rs1" + k].at[i], (dx, dy, dz)))
        return out

    def take_one(e, k, h, copies):
        arrive(copies)
        b, rx, ry, re, rz, zs = (s[n + k] for n in ("B1", "RX1", "RY1", "RE1", "RZ1", "ZS"))
        first = lane((16, 128)) % 16 >= 8

        def beside(dx, dy):
            left = keep(rz[0, 1 + dx, 1 + dy], dx, dy, -1)
            right = roll(keep(rz[1, 1 + dx, 1 + dy], dx, dy, 1), 80)
            return jnp.where(first, left, right)

        for dx in (-1, 0, 1):
            zs[1 + dx, 12:28] = beside(dx, 0)
            zs[1 + dx, 12 - h : 12] = beside(dx, -1)[16 - h : 16]
            zs[1 + dx, 28 : 28 + h] = beside(dx, 1)[0:h]
            count, base, start = (8, 5, 0) if dx == 0 else ((h, 5 - h, 8 - h) if dx < 0 else (h, 13, 0))
            planes = pl.ds(base, count)
            if dx == 0:
                e[planes, 12:28, :] = b[...]
                e[planes, 12 - h : 12, :] = keep(ry[0, :, 8 - h : 8, :], 0, -1, 0)
                e[planes, 28 : 28 + h, :] = keep(ry[1, :, 0:h, :], 0, 1, 0)
            else:
                e[planes, 12:28, :] = keep(rx[side(dx)], dx, 0, 0)
                e[planes, 12 - h : 12, :] = keep(re[side(dx), 0, :, 8 - h : 8, :], dx, -1, 0)
                e[planes, 28 : 28 + h, :] = keep(re[side(dx), 1, :, 0:h, :], dx, 1, 0)
            lo, hi = (8, 32) if h == 4 else (0, 40)
            at = lane((hi - lo, 128))
            halo = ((at >= 24) & (at < 32)) | ((at >= 96) & (at < 104))
            for i in range(count):
                moved = roll(zs[1 + dx, lo:hi], 16 - 16 * (start + i))
                e[base + i, lo:hi, :] = jnp.where(halo, moved, e[base + i, lo:hi, :])

    def send_two(k):
        out = []
        for i, (a, dy, dz) in enumerate(WIDE):
            dst = s["S2" + k].at[gx, 1 - dy, 1 - dz]
            out.append(send(s["PB2" + k], dst, s["ss2" + k].at[i], s["rs2" + k].at[i], (a, dy, dz), (1, 2)))
        s["S2" + k][gx, 1, 1] = s["PB2" + k][...]
        return out

    def take_two(e, k, copies):
        arrive(copies)
        at = lane((8, 128)) // 32
        for x in range(NX):
            for dy in (-1, 0, 1):
                blocks = [keep(s["S2" + k][x, 1 + dy, 1 + dz], 0, dy, dz) for dz in (-1, 0, 1)]
                for p in range(4):
                    val = jnp.zeros((8, 128), F32)
                    for z in range(3):
                        val = jnp.where(at == z, roll(blocks[z], 32 * (z - p)), val)
                    e[1 + 4 * x + p, 16 + 8 * dy : 24 + 8 * dy, :] = val

    def send_core(k):
        to = (gx, gy, gz + 1 - 2 * core)
        return [send(s["PB3" + k], s["S3" + k], s["ss3" + k].at[0], s["rs3" + k].at[0], (0, 0, 0), to=to)]

    def send_chips(k, copies):
        arrive(copies)
        s["YS" + k][...] = s["PB3" + k][...] + s["S3" + k][...]
        out = []
        for i, o in enumerate(CHIPS):
            dst = s["S4" + k].at[gy, gz // 2]
            out.append(send(s["YS" + k], dst, s["ss4" + k].at[i], s["rs4" + k].at[i], o, ()))
        s["S4" + k][gy, gz // 2] = s["YS" + k][...]
        return out

    def take_coarse(dst, base, row, k, copies):
        arrive(copies)
        at = lane((8, 128)) // 32
        for g in range(NY):
            for q in range(4):
                val = jnp.zeros((8, 128), F32)
                for j in range(NZ // 2):
                    val = jnp.where(at == j, roll(s["S4" + k][g, j], 32 * (j - q)), val)
                rows = slice(row + 4 * g, row + 4 * g + 4)
                dst[base + 2 * q, rows, :] = val[0:4]
                dst[base + 2 * q + 1, rows, :] = val[4:8]

    for k, name in ((0, "C0"), (1, "V0")):
        loads[k].wait()
        acc = jnp.zeros((32, 128), F32)
        for p in range(16):
            acc = pack_fine(s[name][p + 1, 8:40, :], k, p, acc)
        s["PZ"][k] = acc
    pl.semaphore_wait(barrier, len(SIX) + len(FAR))

    copies = send_fine(("C0", "V0"), 0)
    loads[2].wait()
    g_ref = s["GV"]
    for name in ("C1", "G1", "EA1", "EB1", "C2", "G2", "EA2", "EB2"):
        s[name][...] = jnp.zeros((18, 40, 128), F32)
    for name in ("C3", "KA", "KB"):
        s[name][...] = jnp.zeros((10, 48, 128), F32)
    s["ZSc"][...] = jnp.zeros((3, 40, 128), F32)
    s["U2"][...] = jnp.zeros((20, 24, 128), F32)
    s["R3"][...] = jnp.zeros((8, 16, 128), F32)
    s["G3"][...] = jnp.zeros((10, 8, 4, 128), F32)
    restrict_fine(lambda p: s["C0"][p + 1, 8:40, :], "c")
    restrict_one(lambda p: s["B1c"][p], 0, "c")
    arrive(copies)
    take_fine("C0", 0)
    weights("0", 16, 32, 1.0, fine_z(0))
    take_fine("V0", 1)

    def sweep_fine(src, dst, zs, k):
        acc = jnp.zeros((32, 128), F32)
        for p in range(16):
            new = swept("0", s[src], p, 32, g_ref[p], zs)
            s[dst][p + 1, 8:40, :] = new
            acc = pack_fine(new, k, p, acc)
        s["PZ"][k] = acc
        return send_fine((dst,), k)

    copies = sweep_fine("V0", "V1", fine_z(1), 2)
    arrive(copies)
    take_fine("V1", 2)
    copies = sweep_fine("V1", "X0", fine_z(2), 3)
    c_one = send_one("c", 5)
    arrive(copies)
    take_fine("X0", 3)
    restrict_fine(lambda p: residual("0", s["X0"], p, 32, g_ref[p], fine_z(3)), "g")

    g_one = send_one("g", 4)
    take_one(s["C1"], "c", 5, c_one)
    c_two = send_two("c")
    weights("1", 16, 24, 0.25, plain_z)
    take_one(s["G1"], "g", 4, g_one)

    def begin(l):
        for p in range(16):
            s["EA" + l][p + 1, 8:32, :] = s["SD" + l][p] * s["G" + l][p + 1, 8:32, :]

    def sweep(l, src, dst):
        for p in range(16):
            right = s["G" + l][p + 1, 8:32, :]
            s[dst][p + 1, 8:32, :] = swept(l, s[src], p, 24, right, plain_z)

    def left(l, src):
        return lambda p: residual(l, s[src], p, 24, s["G" + l][p + 1, 8:32, :], plain_z)

    begin("1")
    sweep("1", "EA1", "EB1")
    rest = left("1", "EB1")
    restrict_one(lambda p: rest(p + 4), 4, "g")

    g_two = send_two("g")
    take_two(s["C2"], "c", c_two)
    restrict_two(lambda p: s["C2"][p + 1, 16:24, :], "c")
    c_core = send_core("c")
    weights("2", 16, 24, 0.0625, plain_z)
    c_chips = send_chips("c", c_core)
    take_two(s["G2"], "g", g_two)
    begin("2")
    sweep("2", "EA2", "EB2")
    rest2 = left("2", "EB2")
    restrict_two(lambda p: rest2(p)[8:16], "g")

    for i, value in enumerate(constants()[0]):
        s["K"][i] = F32(value)
    g_core = send_core("g")
    g_chips = send_chips("g", g_core)
    take_coarse(s["C3"], 1, 8, "c", c_chips)
    weights("3", 8, 32, 0.015625, closed_z)
    at = lane((32, 128))
    for p in range(8):
        inv = F32(1.0) / s["D3"][p]
        s["SD3"][p] = inv
        s["WXM3"][p] = s["WX3"][p] * inv
        s["WXP3"][p] = s["WX3"][p + 1] * inv
        s["WYM3"][p] = s["WY3"][p, 0:32] * inv
        s["WYP3"][p] = s["WY3"][p, 1:33] * inv
        s["WZM3"][p] = jnp.where(at == 0, 0.0, s["WZM3"][p] * inv)
        s["WZP3"][p] = jnp.where(at == 127, 0.0, s["WZP3"][p] * inv)
    take_coarse(s["T3"], 0, 0, "g", g_chips)
    theta = constants()[1]
    for p in range(8):
        t = s["T3"][p] * s["SD3"][p]
        s["T3"][p] = t
        d = t * F32(1.0 / theta)
        s["ST3"][p] = d
        s["KA"][p + 1, 8:40, :] = d

    def cheb(src, dst, i):
        a, b = s["K"][2 * i], s["K"][2 * i + 1]
        v = s[src]
        for p in range(8):
            e = v[p + 1, 8:40, :]
            r = s["T3"][p] - e + s["WXM3"][p] * v[p, 8:40, :] + s["WXP3"][p] * v[p + 2, 8:40, :]
            r = r + s["WYM3"][p] * v[p + 1, 7:39, :] + s["WYP3"][p] * v[p + 1, 9:41, :]
            r = r + s["WZM3"][p] * roll(e, 1) + s["WZP3"][p] * roll(e, -1)
            d = a * s["ST3"][p] + b * r
            s["ST3"][p] = d
            s[dst][p + 1, 8:40, :] = e + d

    def two(i, carry):
        cheb("KA", "KB", 2 * i)
        cheb("KB", "KA", 2 * i + 1)
        return carry

    lax.fori_loop(0, (CHEB - 1) // 2, two, 0)
    cheb("KA", "KB", CHEB - 2)

    for g in range(NY):
        s["G3"][g + 1] = s["KB"][1:9, 8 + 4 * g : 12 + 4 * g, :]
    for j in range(3):
        s["R3"][:, 4 * j : 4 * j + 4, :] = s["G3"][gy + j]
    from_three = picks(lambda r, c: (r == 16 * gz - 16 + c // 2) & (c < 96))
    s["T32"][...] = mm(s["R3"][...].reshape(128, 128), from_three).reshape(8, 16, 128)
    for o in (0, 1):
        s["D32"][:, pl.ds(o, 12, stride=2), :] = s["T32"][:, 0:12, :]
    for p in range(16):
        s["EA2"][p + 1, 8:32, :] = s["EB2"][p + 1, 8:32, :] + s["D32"][p // 2]
    sweep("2", "EA2", "EB2")
    for p in range(16):
        right = s["G2"][p + 1, 8:32, :]
        s["U2"][p + 2] = swept("2", s["EB2"], p, 24, right, plain_z)

    from_two = picks(lambda r, c: (r == 16 + c // 2) & (c >= 24) & (c < 104))
    part = s["U2"][pl.ds(4 * gx, 8)]
    s["T21"][...] = mm(part.reshape(192, 128), from_two).reshape(8, 24, 128)
    for o in (0, 1):
        s["D21"][:, pl.ds(o, 12, stride=2), :] = s["T21"][:, 6:18, :]
    for p in range(16):
        s["EA1"][p + 1, 8:32, :] = s["EB1"][p + 1, 8:32, :] + s["D21"][p // 2]
    sweep("1", "EA1", "EB1")
    sweep("1", "EB1", "EA1")

    from_one = picks(
        lambda r, c: ((c < 128) & (r == 32 + c // 2)) | ((c == 128) & (r == 31)) | ((c == 255) & (r == 96)), 256
    )
    wide = mm(s["EA1"][4:14, 8:32, :].reshape(240, 128), from_one)
    s["TA"][...] = wide[:, 0:128].reshape(10, 24, 128)
    s["TB"][...] = wide[:, 128:256].reshape(10, 24, 128)
    for o in (0, 1):
        s["DA"][:, pl.ds(8 + o, 16, stride=2), :] = s["TA"][:, 4:20, :]
        s["DB"][:, pl.ds(o, 16, stride=2), :] = s["TB"][:, 4:20, :]
    for i in range(18):
        j = (i + 1) // 2
        s["VP"][i, 8:40, :] = s["X0"][i, 8:40, :] + s["DA"][j, 8:40, :]
        if 0 < i < 17:
            s["VP"][i, 7:8, :] = s["X0"][i, 7:8, :] + s["TA"][j, 3:4, :]
            s["VP"][i, 40:41, :] = s["X0"][i, 40:41, :] + s["TA"][j, 20:21, :]
    copies = sweep_fine("VP", "VQ", fine_z(3, lambda p: s["DB"][(p + 2) // 2]), 4)
    arrive(copies)
    take_fine("VQ", 4)
    stores = []
    for p in range(16):
        s["OV"][p] = swept("0", s["VQ"], p, 32, g_ref[p], fine_z(4))
        if p % 4 == 3:
            part = pl.ds(p - 3, 4)
            stores.append(pltpu.make_async_copy(s["OV"].at[part], o_ref.at[part], s["hs"].at[3 + p // 4]))
            stores[-1].start()
    for copy, cond in started:
        when(cond, copy.wait_send)
    for copy in stores:
        copy.wait()


def on_device(right_side, coefficient, guess):
    whole = pl.BlockSpec(memory_space=pl.ANY)
    return pl.pallas_call(
        kernel,
        out_shape=jax.ShapeDtypeStruct((16, 32, 128), F32),
        in_specs=[whole, whole, whole],
        out_specs=whole,
        scratch_shapes=[build_scratch()],
        compiler_params=pltpu.CompilerParams(
            collective_id=0, has_side_effects=True, vmem_limit_bytes=56 * 2**20
        ),
    )(right_side, coefficient, guess)


def solution(mesh):
    spec = P("gx", "gy", "gz")
    return jax.shard_map(on_device, mesh=mesh, in_specs=(spec, spec, spec), out_specs=spec, check_vma=False)
```

```python
import itertools

import jax
import jax.numpy as jnp
import numpy as np
from jax import lax
from jax.experimental import pallas as pl
from jax.experimental.pallas import tpu as pltpu
from jax.sharding import PartitionSpec as P

CHEB = 20
OMEGA = 2.0 / 3.0
CHEB_LOW = 0.1
CHEB_HIGH = 2.0
MESH = pl.DeviceIdType.MESH
F32 = jnp.float32
NX, NY, NZ = 4, 8, 8
SIX = ((1, 0, 0), (-1, 0, 0), (0, 1, 0), (0, -1, 0), (0, 0, 1), (0, 0, -1))
AROUND = sorted(
    (o for o in itertools.product((-1, 0, 1), repeat=3) if o != (0, 0, 0)),
    key=lambda o: -(abs(o[0]) + abs(o[1]) + abs(o[2])),
)
WIDE = sorted(
    (o for o in itertools.product(range(NX), (-1, 0, 1), (-1, 0, 1)) if o != (0, 0, 0)),
    key=lambda o: -((o[0] != 0) + (o[0] == 2) + abs(o[1]) + abs(o[2])),
)
CHIPS = sorted(
    (o for o in itertools.product((0,), range(NY), range(0, NZ, 2)) if o != (0, 0, 0)),
    key=lambda o: -(min(o[1], NY - o[1]) + min(o[2], NZ - o[2]) // 2),
)

def side(d):
    return 0 if d < 0 else 1


def constants():
    theta, delta = 0.5 * (CHEB_HIGH + CHEB_LOW), 0.5 * (CHEB_HIGH - CHEB_LOW)
    sigma = theta / delta
    rho, out = np.float32(1.0 / sigma), []
    for _ in range(CHEB - 1):
        rho_next = np.float32(1.0 / (2.0 * sigma - rho))
        out += [np.float32(rho_next * rho), np.float32(2.0 * rho_next / delta)]
        rho = rho_next
    return np.array(out, np.float32), theta


def lane(shape):
    return lax.broadcasted_iota(jnp.int32, shape, len(shape) - 1)


def roll(x, by):
    return pltpu.roll(x, by % 128, x.ndim - 1)


def mm(x, m):
    return lax.dot_general(
        x, m, (((1,), (0,)), ((), ())), precision=lax.Precision.HIGHEST, preferred_element_type=F32
    )


def picks(condition, width=128, value=1.0):
    row = lax.broadcasted_iota(jnp.int32, (128, width), 0)
    col = lax.broadcasted_iota(jnp.int32, (128, width), 1)
    return jnp.where(condition(row, col), F32(value), F32(0.0))


def vm(*shape):
    return pltpu.VMEM(shape, F32)


def dma(*shape):
    return pltpu.SemaphoreType.DMA(shape)


def build_scratch():
    s = {}
    for name in ("C0", "V0", "V1", "X0", "VP", "VQ"):
        s[name] = vm(18, 48, 128)
    s.update(WX0=vm(17, 32, 128), WY0=vm(16, 40, 128))
    for name in ("WZM0", "WZP0", "D0", "SD0"):
        s[name] = vm(16, 32, 128)
    s.update(
        YB=vm(2, 5, 16, 1, 128), PZ=vm(5, 32, 128),
        RX=vm(5, 2, 32, 128), RY=vm(2, 5, 16, 1, 128), RZ=vm(2, 5, 32, 128), MZ=vm(5, 32, 128),
        ss0=dma(5, 6), rs0=dma(5, 6), hs=dma(8), GV=vm(16, 32, 128), OV=vm(16, 32, 128),
    )
    s.update(RS0=vm(8, 32, 128), RS1=vm(4, 24, 128), RS2=vm(8, 8, 128), QS=vm(4, 8, 128))
    for k, h in (("c", 5), ("g", 4)):
        s["B1" + k] = vm(8, 16, 128)
        s["PZ1" + k] = vm(16, 128)
        s["RX1" + k] = vm(2, h, 16, 128)
        s["RY1" + k] = vm(2, 8, 8, 128)
        s["RE1" + k] = vm(2, 2, h, 8, 128)
        s["RZ1" + k] = vm(2, 3, 3, 16, 128)
        s["ss1" + k], s["rs1" + k] = dma(26), dma(26)
        s["ZS" + k] = vm(3, 40, 128)
        s["PB2" + k] = vm(8, 128)
        s["S2" + k] = vm(NX, 3, 3, 8, 128)
        s["ss2" + k], s["rs2" + k] = dma(len(WIDE)), dma(len(WIDE))
        s["PB3" + k] = vm(8, 128)
        s["S3" + k] = vm(8, 128)
        s["YS" + k] = vm(8, 128)
        s["S4" + k] = vm(NY, NZ // 2, 8, 128)
        s["ss3" + k], s["rs3" + k] = dma(1), dma(1)
        s["ss4" + k], s["rs4" + k] = dma(len(CHIPS)), dma(len(CHIPS))
    for l in ("1", "2"):
        for name in ("C", "G", "EA", "EB"):
            s[name + l] = vm(18, 40, 128)
        s.update({"WX" + l: vm(17, 24, 128), "WY" + l: vm(16, 32, 128)})
        for name in ("WZM", "WZP", "D", "SD"):
            s[name + l] = vm(16, 24, 128)
    s["wrap"] = pltpu.SemaphoreType.REGULAR((3, 3))
    s["K"] = pltpu.SMEM((2 * (CHEB - 1),), F32)
    s.update(U2=vm(20, 24, 128), T21=vm(8, 24, 128), D21=vm(8, 24, 128))
    s.update(TA=vm(10, 24, 128), TB=vm(10, 24, 128), DA=vm(10, 48, 128), DB=vm(10, 32, 128))
    s.update(C3=vm(10, 48, 128), T3=vm(8, 32, 128), KA=vm(10, 48, 128), KB=vm(10, 48, 128), ST3=vm(8, 32, 128))
    s.update(WX3=vm(9, 32, 128), WY3=vm(8, 40, 128))
    for name in ("WXM3", "WXP3", "WYM3", "WYP3", "WZM3", "WZP3", "D3", "SD3"):
        s[name] = vm(8, 32, 128)
    s.update(G3=vm(10, 8, 4, 128), R3=vm(8, 16, 128), T32=vm(8, 16, 128), D32=vm(8, 24, 128))
    return s


def kernel(g_hbm, c_hbm, v_hbm, o_ref, s):
    gx, gy, gz = (lax.axis_index(a) for a in ("gx", "gy", "gz"))
    here = {
        0: {-1: gx > 0, 1: gx < NX - 1},
        1: {-1: gy > 0, 1: gy < NY - 1},
        2: {-1: gz > 0, 1: gz < NZ - 1},
    }
    core = lax.rem(gz, 2)
    started = []

    def exists(o, axes=(0, 1, 2)):
        cond = None
        for axis in axes:
            if o[axis]:
                cond = here[axis][o[axis]] if cond is None else cond & here[axis][o[axis]]
        return cond

    def keep(x, *o, axes=(0, 1, 2)):
        cond = exists(o, axes)
        return x if cond is None else jnp.where(cond, x, 0.0)

    def when(cond, act):
        if cond is None:
            act()
        else:
            pl.when(cond)(act)

    def target(o):
        return (lax.rem(gx + o[0] + NX, NX), lax.rem(gy + o[1] + NY, NY), lax.rem(gz + o[2] + NZ, NZ))

    def send(src, dst, ss, rs, o, axes=(0, 1, 2), to=None):
        copy = pltpu.make_async_remote_copy(
            src_ref=src, dst_ref=dst, send_sem=ss, recv_sem=rs,
            device_id=target(o) if to is None else to, device_id_type=MESH,
        )
        out = exists(o, axes)
        when(out, copy.start)
        started.append((copy, out))
        return copy, exists(tuple(-d for d in o), axes)

    def edges(o):
        axis = next(i for i in range(3) if o[i])
        return jnp.logical_not(here[axis][o[axis]]), s["wrap"], axis

    def tell_edges(k):
        for o in SIX:
            cond, sem, axis = edges(o)
            when(cond, lambda: pl.semaphore_signal(
                sem.at[k, axis], inc=1, device_id=target(o), device_id_type=MESH))

    def hear_edges(k):
        for o in SIX:
            cond, sem, axis = edges(o)
            when(cond, lambda: pl.semaphore_wait(sem.at[k, axis], 1))

    def arrive(copies):
        for copy, cond in copies:
            when(cond, copy.wait_recv)

    barrier = pltpu.get_barrier_semaphore()
    for o in SIX:
        pl.semaphore_signal(barrier, inc=1, device_id=target(o), device_id_type=MESH)
    main = (pl.ds(1, 16), pl.ds(8, 32))
    loads = [
        pltpu.make_async_copy(c_hbm, s["C0"].at[main], s["hs"].at[0]),
        pltpu.make_async_copy(v_hbm, s["V0"].at[main], s["hs"].at[1]),
        pltpu.make_async_copy(g_hbm, s["GV"], s["hs"].at[2]),
    ]
    for load in loads:
        load.start()

    def pack_fine(plane, k, p, acc):
        s["YB"][0, k, p] = plane[0:1]
        s["YB"][1, k, p] = plane[31:32]
        at = lane((32, 128))
        mine = (at == (2 * p) % 128) | (at == (2 * p - 1) % 128)
        return jnp.where(mine, roll(plane, 2 * p), acc)

    def send_fine(names, k):
        out = []
        ss, rs = s["ss0"], s["rs0"]
        yb, rx, ry, rz, pz = s["YB"], s["RX"], s["RY"], s["RZ"], s["PZ"]
        ks = pl.ds(k, len(names))
        out.append(send(yb.at[1, ks], ry.at[0, ks], ss.at[k, 0], rs.at[k, 0], (0, 1, 0)))
        out.append(send(yb.at[0, ks], ry.at[1, ks], ss.at[k, 1], rs.at[k, 1], (0, -1, 0)))
        for i, name in enumerate(names):
            low, high = s[name].at[1, pl.ds(8, 32)], s[name].at[16, pl.ds(8, 32)]
            out.append(send(high, rx.at[k + i, 0], ss.at[k + i, 2], rs.at[k + i, 2], (1, 0, 0)))
            out.append(send(low, rx.at[k + i, 1], ss.at[k + i, 3], rs.at[k + i, 3], (-1, 0, 0)))
        out.append(send(pz.at[ks], rz.at[0, ks], ss.at[k, 4], rs.at[k, 4], (0, 0, 1)))
        out.append(send(pz.at[ks], rz.at[1, ks], ss.at[k, 5], rs.at[k, 5], (0, 0, -1)))
        return out

    def take_fine(name, k):
        v = s[name]
        v[0, 8:40, :] = keep(s["RX"][k, 0], -1, 0, 0)
        v[17, 8:40, :] = keep(s["RX"][k, 1], 1, 0, 0)
        v[1:17, 7:8, :] = keep(s["RY"][0, k], 0, -1, 0)
        v[1:17, 40:41, :] = keep(s["RY"][1, k], 0, 1, 0)
        odd = lane((32, 128)) % 2 == 1
        right, left = keep(s["RZ"][1, k], 0, 0, 1), keep(s["RZ"][0, k], 0, 0, -1)
        s["MZ"][k] = jnp.where(odd, roll(right, -1), roll(left, 1))

    def fine_z(k, extra=None):
        def get(p, v):
            at = lane((32, 128))
            edge = roll(s["MZ"][k], -2 * p)
            if extra is not None:
                edge = edge + extra(p)
            return jnp.where(at == 0, edge, roll(v, 1)), jnp.where(at == 127, edge, roll(v, -1))

        return get

    def plain_z(p, v):
        return roll(v, 1), roll(v, -1)

    def closed_z(p, v):
        at = lane(v.shape)
        return jnp.where(at == 0, 0.0, roll(v, 1)), jnp.where(at == 127, 0.0, roll(v, -1))

    def weights(l, n, rows, scale, zs):
        c, wx, wy = s["C" + l], s["WX" + l], s["WY" + l]
        h = F32(0.5 * scale)
        for p in range(n + 1):
            wx[p] = h * (c[p, 8 : 8 + rows, :] + c[p + 1, 8 : 8 + rows, :])
        for p in range(n):
            wy[p] = h * (c[p + 1, 8 : 16 + rows, :] + c[p + 1, 7 : 15 + rows, :])
            mid = c[p + 1, 8 : 8 + rows, :]
            zm, zp = zs(p, mid)
            wzm, wzp = h * (mid + zm), h * (mid + zp)
            d = wx[p] + wx[p + 1] + wy[p, 0:rows] + wy[p, 1 : rows + 1] + wzm + wzp
            s["WZM" + l][p], s["WZP" + l][p], s["D" + l][p] = wzm, wzp, d
            s["SD" + l][p] = jnp.where(mid > 0, F32(OMEGA) / d, 0.0)

    def gathered(l, v, p, rows, right, zs):
        wx, wy = s["WX" + l], s["WY" + l]
        mid = v[p + 1, 8 : 8 + rows, :]
        zm, zp = zs(p, mid)
        total = right + wx[p] * v[p, 8 : 8 + rows, :] + wx[p + 1] * v[p + 2, 8 : 8 + rows, :]
        total = total + wy[p, 0:rows] * v[p + 1, 7 : 7 + rows, :]
        total = total + wy[p, 1 : rows + 1] * v[p + 1, 9 : 9 + rows, :]
        total = total + s["WZM" + l][p] * zm + s["WZP" + l][p] * zp
        return mid, total

    def swept(l, v, p, rows, right, zs):
        mid, total = gathered(l, v, p, rows, right, zs)
        return mid * F32(1.0 - OMEGA) + s["SD" + l][p] * total

    def residual(l, v, p, rows, right, zs):
        mid, total = gathered(l, v, p, rows, right, zs)
        return total - s["D" + l][p] * mid

    to_one = picks(lambda r, c: r // 2 + 32 == c, value=0.125)
    to_two = [
        picks(lambda r, c, p=p: (c // 32 == p) & (r // 2 == c % 32 + 16), value=0.125) for p in range(4)
    ]
    to_three = [
        picks(lambda r, c, q=q: (c // 16 == 2 * q + core) & (r // 2 == c % 16 + 16), value=0.125)
        for q in range(4)
    ]

    def restrict_fine(plane, k):
        rs = s["RS0"]
        for q in range(8):
            rs[q] = plane(2 * q) + plane(2 * q + 1)
        half = rs[:, pl.ds(0, 16, stride=2), :] + rs[:, pl.ds(1, 16, stride=2), :]
        block = mm(half.reshape(128, 128), to_one).reshape(8, 16, 128)
        s["B1" + k][...] = block
        at = lane((16, 128))
        acc = jnp.zeros((16, 128), F32)
        for p in range(8):
            acc = jnp.where((at >= 16 * p) & (at < 16 * p + 8), roll(block[p], 16 * p - 32), acc)
            acc = jnp.where((at >= 16 * p + 8) & (at < 16 * p + 16), roll(block[p], 16 * p + 8 - 88), acc)
        s["PZ1" + k][...] = acc

    def restrict_one(plane, first, k):
        rs = s["RS1"]
        rows = 24 if first == 4 else 16
        for q in range(4):
            rs[q, 0:rows] = plane(2 * q) + plane(2 * q + 1)
        half = rs[:, pl.ds(first, 8, stride=2), :] + rs[:, pl.ds(first + 1, 8, stride=2), :]
        s["PB2" + k][...] = sum(mm(half[p], to_two[p]) for p in range(4))

    def restrict_two(plane, k):
        rs, qs = s["RS2"], s["QS"]
        for q in range(8):
            rs[q] = plane(2 * q) + plane(2 * q + 1)
        half = rs[:, pl.ds(0, 4, stride=2), :] + rs[:, pl.ds(1, 4, stride=2), :]
        for q in range(4):
            qs[q, 0:4] = half[2 * q]
            qs[q, 4:8] = half[2 * q + 1]
        s["PB3" + k][...] = sum(mm(qs[q], to_three[q]) for q in range(4))

    def send_one(k, h, axes=(0, 1, 2)):
        out = []
        b, pz = s["B1" + k], s["PZ1" + k]
        for i, (dx, dy, dz) in enumerate(AROUND):
            if dz:
                src, dst = pz, s["RZ1" + k].at[side(-dz), 1 - dx, 1 - dy]
            else:
                xs = pl.ds(8 - h, h) if dx > 0 else pl.ds(0, h)
                ys = pl.ds(8, 8) if dy > 0 else pl.ds(0, 8)
                if dx and dy:
                    src, dst = b.at[xs, ys], s["RE1" + k].at[side(-dx), side(-dy)]
                elif dx:
                    src, dst = b.at[xs], s["RX1" + k].at[side(-dx)]
                else:
                    src, dst = b.at[:, ys], s["RY1" + k].at[side(-dy)]
            out.append(send(src, dst, s["ss1" + k].at[i], s["rs1" + k].at[i], (dx, dy, dz), axes))
        return out

    def take_one(e, k, h, copies):
        arrive(copies)
        b, rx, ry, re, rz, zs = (s[n + k] for n in ("B1", "RX1", "RY1", "RE1", "RZ1", "ZS"))
        first = lane((16, 128)) % 16 >= 8

        def beside(dx, dy):
            left = keep(rz[0, 1 + dx, 1 + dy], dx, dy, -1)
            right = roll(keep(rz[1, 1 + dx, 1 + dy], dx, dy, 1), 80)
            return jnp.where(first, left, right)

        for dx in (-1, 0, 1):
            zs[1 + dx, 12:28] = beside(dx, 0)
            zs[1 + dx, 12 - h : 12] = beside(dx, -1)[16 - h : 16]
            zs[1 + dx, 28 : 28 + h] = beside(dx, 1)[0:h]
            count, base, start = (8, 5, 0) if dx == 0 else ((h, 5 - h, 8 - h) if dx < 0 else (h, 13, 0))
            planes = pl.ds(base, count)
            if dx == 0:
                e[planes, 12:28, :] = b[...]
                e[planes, 12 - h : 12, :] = keep(ry[0, :, 8 - h : 8, :], 0, -1, 0)
                e[planes, 28 : 28 + h, :] = keep(ry[1, :, 0:h, :], 0, 1, 0)
            else:
                e[planes, 12:28, :] = keep(rx[side(dx)], dx, 0, 0)
                e[planes, 12 - h : 12, :] = keep(re[side(dx), 0, :, 8 - h : 8, :], dx, -1, 0)
                e[planes, 28 : 28 + h, :] = keep(re[side(dx), 1, :, 0:h, :], dx, 1, 0)
            lo, hi = (8, 32) if h == 4 else (0, 40)
            at = lane((hi - lo, 128))
            halo = ((at >= 24) & (at < 32)) | ((at >= 96) & (at < 104))
            for i in range(count):
                moved = roll(zs[1 + dx, lo:hi], 16 - 16 * (start + i))
                e[base + i, lo:hi, :] = jnp.where(halo, moved, e[base + i, lo:hi, :])

    def send_two(k, axes=(1, 2)):
        out = []
        for i, (a, dy, dz) in enumerate(WIDE):
            dst = s["S2" + k].at[gx, 1 - dy, 1 - dz]
            out.append(send(s["PB2" + k], dst, s["ss2" + k].at[i], s["rs2" + k].at[i], (a, dy, dz), axes))
        s["S2" + k][gx, 1, 1] = s["PB2" + k][...]
        return out

    def take_two(e, k, copies):
        arrive(copies)
        at = lane((8, 128)) // 32
        for x in range(NX):
            for dy in (-1, 0, 1):
                blocks = [keep(s["S2" + k][x, 1 + dy, 1 + dz], 0, dy, dz) for dz in (-1, 0, 1)]
                for p in range(4):
                    val = jnp.zeros((8, 128), F32)
                    for z in range(3):
                        val = jnp.where(at == z, roll(blocks[z], 32 * (z - p)), val)
                    e[1 + 4 * x + p, 16 + 8 * dy : 24 + 8 * dy, :] = val

    def send_core(k):
        to = (gx, gy, gz + 1 - 2 * core)
        return [send(s["PB3" + k], s["S3" + k], s["ss3" + k].at[0], s["rs3" + k].at[0], (0, 0, 0), to=to)]

    def send_chips(k, copies):
        arrive(copies)
        s["YS" + k][...] = s["PB3" + k][...] + s["S3" + k][...]
        out = []
        for i, o in enumerate(CHIPS):
            dst = s["S4" + k].at[gy, gz // 2]
            out.append(send(s["YS" + k], dst, s["ss4" + k].at[i], s["rs4" + k].at[i], o, ()))
        s["S4" + k][gy, gz // 2] = s["YS" + k][...]
        return out

    def take_coarse(dst, base, row, k, copies):
        arrive(copies)
        at = lane((8, 128)) // 32
        for g in range(NY):
            for q in range(4):
                val = jnp.zeros((8, 128), F32)
                for j in range(NZ // 2):
                    val = jnp.where(at == j, roll(s["S4" + k][g, j], 32 * (j - q)), val)
                rows = slice(row + 4 * g, row + 4 * g + 4)
                dst[base + 2 * q, rows, :] = val[0:4]
                dst[base + 2 * q + 1, rows, :] = val[4:8]

    for k, name in ((0, "C0"), (1, "V0")):
        loads[k].wait()
        acc = jnp.zeros((32, 128), F32)
        for p in range(16):
            acc = pack_fine(s[name][p + 1, 8:40, :], k, p, acc)
        s["PZ"][k] = acc
    pl.semaphore_wait(barrier, len(SIX))

    copies = send_fine(("C0", "V0"), 0)
    tell_edges(0)
    loads[2].wait()
    g_ref = s["GV"]
    for name in ("C1", "G1", "EA1", "EB1", "C2", "G2", "EA2", "EB2"):
        s[name][...] = jnp.zeros((18, 40, 128), F32)
    for name in ("C3", "KA", "KB"):
        s[name][...] = jnp.zeros((10, 48, 128), F32)
    s["ZSc"][...] = jnp.zeros((3, 40, 128), F32)
    s["U2"][...] = jnp.zeros((20, 24, 128), F32)
    s["R3"][...] = jnp.zeros((8, 16, 128), F32)
    s["G3"][...] = jnp.zeros((10, 8, 4, 128), F32)
    restrict_fine(lambda p: s["C0"][p + 1, 8:40, :], "c")
    restrict_one(lambda p: s["B1c"][p], 0, "c")
    arrive(copies)
    hear_edges(0)
    take_fine("C0", 0)
    weights("0", 16, 32, 1.0, fine_z(0))
    take_fine("V0", 1)

    def sweep_fine(src, dst, zs, k):
        acc = jnp.zeros((32, 128), F32)
        for p in range(16):
            new = swept("0", s[src], p, 32, g_ref[p], zs)
            s[dst][p + 1, 8:40, :] = new
            acc = pack_fine(new, k, p, acc)
        s["PZ"][k] = acc
        return send_fine((dst,), k)

    copies = sweep_fine("V0", "V1", fine_z(1), 2)
    tell_edges(1)
    arrive(copies)
    hear_edges(1)
    take_fine("V1", 2)
    copies = sweep_fine("V1", "X0", fine_z(2), 3)
    tell_edges(2)
    c_one = send_one("c", 5, ())
    arrive(copies)
    hear_edges(2)
    take_fine("X0", 3)
    restrict_fine(lambda p: residual("0", s["X0"], p, 32, g_ref[p], fine_z(3)), "g")

    g_one = send_one("g", 4)
    take_one(s["C1"], "c", 5, c_one)
    c_two = send_two("c", ())
    weights("1", 16, 24, 0.25, plain_z)
    take_one(s["G1"], "g", 4, g_one)

    def begin(l):
        for p in range(16):
            s["EA" + l][p + 1, 8:32, :] = s["SD" + l][p] * s["G" + l][p + 1, 8:32, :]

    def sweep(l, src, dst):
        for p in range(16):
            right = s["G" + l][p + 1, 8:32, :]
            s[dst][p + 1, 8:32, :] = swept(l, s[src], p, 24, right, plain_z)

    def left(l, src):
        return lambda p: residual(l, s[src], p, 24, s["G" + l][p + 1, 8:32, :], plain_z)

    begin("1")
    sweep("1", "EA1", "EB1")
    rest = left("1", "EB1")
    restrict_one(lambda p: rest(p + 4), 4, "g")

    g_two = send_two("g")
    take_two(s["C2"], "c", c_two)
    restrict_two(lambda p: s["C2"][p + 1, 16:24, :], "c")
    c_core = send_core("c")
    weights("2", 16, 24, 0.0625, plain_z)
    c_chips = send_chips("c", c_core)
    take_two(s["G2"], "g", g_two)
    begin("2")
    sweep("2", "EA2", "EB2")
    rest2 = left("2", "EB2")
    restrict_two(lambda p: rest2(p)[8:16], "g")

    for i, value in enumerate(constants()[0]):
        s["K"][i] = F32(value)
    g_core = send_core("g")
    g_chips = send_chips("g", g_core)
    take_coarse(s["C3"], 1, 8, "c", c_chips)
    weights("3", 8, 32, 0.015625, closed_z)
    at = lane((32, 128))
    for p in range(8):
        inv = F32(1.0) / s["D3"][p]
        s["SD3"][p] = inv
        s["WXM3"][p] = s["WX3"][p] * inv
        s["WXP3"][p] = s["WX3"][p + 1] * inv
        s["WYM3"][p] = s["WY3"][p, 0:32] * inv
        s["WYP3"][p] = s["WY3"][p, 1:33] * inv
        s["WZM3"][p] = jnp.where(at == 0, 0.0, s["WZM3"][p] * inv)
        s["WZP3"][p] = jnp.where(at == 127, 0.0, s["WZP3"][p] * inv)
    take_coarse(s["T3"], 0, 0, "g", g_chips)
    theta = constants()[1]
    for p in range(8):
        t = s["T3"][p] * s["SD3"][p]
        s["T3"][p] = t
        d = t * F32(1.0 / theta)
        s["ST3"][p] = d
        s["KA"][p + 1, 8:40, :] = d

    def cheb(src, dst, i):
        a, b = s["K"][2 * i], s["K"][2 * i + 1]
        v = s[src]
        for p in range(8):
            e = v[p + 1, 8:40, :]
            r = s["T3"][p] - e + s["WXM3"][p] * v[p, 8:40, :] + s["WXP3"][p] * v[p + 2, 8:40, :]
            r = r + s["WYM3"][p] * v[p + 1, 7:39, :] + s["WYP3"][p] * v[p + 1, 9:41, :]
            r = r + s["WZM3"][p] * roll(e, 1) + s["WZP3"][p] * roll(e, -1)
            d = a * s["ST3"][p] + b * r
            s["ST3"][p] = d
            s[dst][p + 1, 8:40, :] = e + d

    def two(i, carry):
        cheb("KA", "KB", 2 * i)
        cheb("KB", "KA", 2 * i + 1)
        return carry

    lax.fori_loop(0, (CHEB - 1) // 2, two, 0)
    cheb("KA", "KB", CHEB - 2)

    for g in range(NY):
        s["G3"][g + 1] = s["KB"][1:9, 8 + 4 * g : 12 + 4 * g, :]
    for j in range(3):
        s["R3"][:, 4 * j : 4 * j + 4, :] = s["G3"][gy + j]
    from_three = picks(lambda r, c: (r == 16 * gz - 16 + c // 2) & (c < 96))
    s["T32"][...] = mm(s["R3"][...].reshape(128, 128), from_three).reshape(8, 16, 128)
    for o in (0, 1):
        s["D32"][:, pl.ds(o, 12, stride=2), :] = s["T32"][:, 0:12, :]
    for p in range(16):
        s["EA2"][p + 1, 8:32, :] = s["EB2"][p + 1, 8:32, :] + s["D32"][p // 2]
    sweep("2", "EA2", "EB2")
    for p in range(16):
        right = s["G2"][p + 1, 8:32, :]
        s["U2"][p + 2] = swept("2", s["EB2"], p, 24, right, plain_z)

    from_two = picks(lambda r, c: (r == 16 + c // 2) & (c >= 24) & (c < 104))
    part = s["U2"][pl.ds(4 * gx, 8)]
    s["T21"][...] = mm(part.reshape(192, 128), from_two).reshape(8, 24, 128)
    for o in (0, 1):
        s["D21"][:, pl.ds(o, 12, stride=2), :] = s["T21"][:, 6:18, :]
    for p in range(16):
        s["EA1"][p + 1, 8:32, :] = s["EB1"][p + 1, 8:32, :] + s["D21"][p // 2]
    sweep("1", "EA1", "EB1")
    sweep("1", "EB1", "EA1")

    from_one = picks(
        lambda r, c: ((c < 128) & (r == 32 + c // 2)) | ((c == 128) & (r == 31)) | ((c == 255) & (r == 96)), 256
    )
    wide = mm(s["EA1"][4:14, 8:32, :].reshape(240, 128), from_one)
    s["TA"][...] = wide[:, 0:128].reshape(10, 24, 128)
    s["TB"][...] = wide[:, 128:256].reshape(10, 24, 128)
    for o in (0, 1):
        s["DA"][:, pl.ds(8 + o, 16, stride=2), :] = s["TA"][:, 4:20, :]
        s["DB"][:, pl.ds(o, 16, stride=2), :] = s["TB"][:, 4:20, :]
    for i in range(18):
        j = (i + 1) // 2
        s["VP"][i, 8:40, :] = s["X0"][i, 8:40, :] + s["DA"][j, 8:40, :]
        if 0 < i < 17:
            s["VP"][i, 7:8, :] = s["X0"][i, 7:8, :] + s["TA"][j, 3:4, :]
            s["VP"][i, 40:41, :] = s["X0"][i, 40:41, :] + s["TA"][j, 20:21, :]
    copies = sweep_fine("VP", "VQ", fine_z(3, lambda p: s["DB"][(p + 2) // 2]), 4)
    arrive(copies)
    take_fine("VQ", 4)
    stores = []
    for p in range(16):
        s["OV"][p] = swept("0", s["VQ"], p, 32, g_ref[p], fine_z(4))
        if p % 4 == 3:
            part = pl.ds(p - 3, 4)
            stores.append(pltpu.make_async_copy(s["OV"].at[part], o_ref.at[part], s["hs"].at[3 + p // 4]))
            stores[-1].start()
    for copy, cond in started:
        when(cond, copy.wait_send)
    for copy in stores:
        copy.wait()


def on_device(right_side, coefficient, guess):
    whole = pl.BlockSpec(memory_space=pl.ANY)
    return pl.pallas_call(
        kernel,
        out_shape=jax.ShapeDtypeStruct((16, 32, 128), F32),
        in_specs=[whole, whole, whole],
        out_specs=whole,
        scratch_shapes=[build_scratch()],
        compiler_params=pltpu.CompilerParams(
            collective_id=0, has_side_effects=True, vmem_limit_bytes=56 * 2**20
        ),
    )(right_side, coefficient, guess)


def solution(mesh):
    spec = P("gx", "gy", "gz")
    return jax.shard_map(on_device, mesh=mesh, in_specs=(spec, spec, spec), out_specs=spec, check_vma=False)
```

```python
import itertools

import jax
import jax.numpy as jnp
import numpy as np
from jax import lax
from jax.experimental import pallas as pl
from jax.experimental.pallas import tpu as pltpu
from jax.sharding import PartitionSpec as P

CHEB = 20
OMEGA = 2.0 / 3.0
CHEB_LOW = 0.1
CHEB_HIGH = 2.0
MESH = pl.DeviceIdType.MESH
F32 = jnp.float32
NX, NY, NZ = 4, 8, 8
SIX = ((1, 0, 0), (-1, 0, 0), (0, 1, 0), (0, -1, 0), (0, 0, 1), (0, 0, -1))
AROUND = sorted(
    (o for o in itertools.product((-1, 0, 1), repeat=3) if o != (0, 0, 0)),
    key=lambda o: -(abs(o[0]) + abs(o[1]) + abs(o[2])),
)
WIDE = sorted(
    (o for o in itertools.product(range(NX), (-1, 0, 1), (-1, 0, 1)) if o != (0, 0, 0)),
    key=lambda o: -((o[0] != 0) + (o[0] == 2) + abs(o[1]) + abs(o[2])),
)
CHIPS = sorted(
    (o for o in itertools.product((0,), range(NY), range(0, NZ, 2)) if o != (0, 0, 0)),
    key=lambda o: -(min(o[1], NY - o[1]) + min(o[2], NZ - o[2]) // 2),
)

def side(d):
    return 0 if d < 0 else 1


def constants():
    theta, delta = 0.5 * (CHEB_HIGH + CHEB_LOW), 0.5 * (CHEB_HIGH - CHEB_LOW)
    sigma = theta / delta
    rho, out = np.float32(1.0 / sigma), []
    for _ in range(CHEB - 1):
        rho_next = np.float32(1.0 / (2.0 * sigma - rho))
        out += [np.float32(rho_next * rho), np.float32(2.0 * rho_next / delta)]
        rho = rho_next
    return np.array(out, np.float32), theta


def lane(shape):
    return lax.broadcasted_iota(jnp.int32, shape, len(shape) - 1)


def roll(x, by):
    return pltpu.roll(x, by % 128, x.ndim - 1)


def mm(x, m):
    return lax.dot_general(
        x, m, (((1,), (0,)), ((), ())), precision=lax.Precision.HIGHEST, preferred_element_type=F32
    )


def picks(condition, width=128, value=1.0):
    row = lax.broadcasted_iota(jnp.int32, (128, width), 0)
    col = lax.broadcasted_iota(jnp.int32, (128, width), 1)
    return jnp.where(condition(row, col), F32(value), F32(0.0))


def vm(*shape):
    return pltpu.VMEM(shape, F32)


def dma(*shape):
    return pltpu.SemaphoreType.DMA(shape)


def build_scratch():
    s = {}
    for name in ("C0", "V0", "V1", "X0", "VP", "VQ"):
        s[name] = vm(18, 48, 128)
    s.update(WX0=vm(17, 32, 128), WY0=vm(16, 40, 128))
    for name in ("WZM0", "WZP0", "D0", "SD0"):
        s[name] = vm(16, 32, 128)
    s.update(
        YB=vm(2, 5, 16, 1, 128), PZ=vm(5, 32, 128),
        RX=vm(5, 2, 32, 128), RY=vm(2, 5, 16, 1, 128), RZ=vm(2, 5, 32, 128), MZ=vm(5, 32, 128),
        ss=dma(65), rs=dma(65), W=vm(92, 8, 128), hs=dma(8), GV=vm(16, 32, 128), OV=vm(16, 32, 128),
    )
    s.update(RS0=vm(8, 32, 128), RS1=vm(4, 24, 128), RS2=vm(8, 8, 128), QS=vm(4, 8, 128))
    for k, h in (("c", 5), ("g", 4)):
        s["B1" + k] = vm(8, 16, 128)
        s["PZ1" + k] = vm(16, 128)
        s["RX1" + k] = vm(2, h, 16, 128)
        s["RY1" + k] = vm(2, 8, 8, 128)
        s["RE1" + k] = vm(2, 2, h, 8, 128)
        s["RZ1" + k] = vm(2, 3, 3, 16, 128)
        s["ZS" + k] = vm(3, 40, 128)
        s["PB2" + k] = vm(8, 128)
        s["S2" + k] = vm(NX, 3, 3, 8, 128)
        s["PB3" + k] = vm(8, 128)
        s["S3" + k] = vm(8, 128)
        s["YS" + k] = vm(8, 128)
        s["S4" + k] = vm(NY, NZ // 2, 8, 128)
    for l in ("1", "2"):
        for name in ("C", "G", "EA", "EB"):
            s[name + l] = vm(18, 40, 128)
        s.update({"WX" + l: vm(17, 24, 128), "WY" + l: vm(16, 32, 128)})
        for name in ("WZM", "WZP", "D", "SD"):
            s[name + l] = vm(16, 24, 128)
    s["wrap"] = pltpu.SemaphoreType.REGULAR((3,))
    s["K"] = pltpu.SMEM((2 * (CHEB - 1),), F32)
    s.update(U2=vm(20, 24, 128), T21=vm(8, 24, 128), D21=vm(8, 24, 128))
    s.update(TA=vm(10, 24, 128), TB=vm(10, 24, 128), DA=vm(10, 48, 128), DB=vm(10, 32, 128))
    s.update(C3=vm(10, 48, 128), T3=vm(8, 32, 128), KA=vm(10, 48, 128), KB=vm(10, 48, 128), ST3=vm(8, 32, 128))
    s.update(WX3=vm(9, 32, 128), WY3=vm(8, 40, 128))
    for name in ("WXM3", "WXP3", "WYM3", "WYP3", "WZM3", "WZP3", "D3", "SD3"):
        s[name] = vm(8, 32, 128)
    s.update(G3=vm(10, 8, 4, 128), R3=vm(8, 16, 128), T32=vm(8, 16, 128), D32=vm(8, 24, 128))
    return s


def kernel(g_hbm, c_hbm, v_hbm, o_ref, s):
    gx, gy, gz = (lax.axis_index(a) for a in ("gx", "gy", "gz"))
    here = {
        0: {-1: gx > 0, 1: gx < NX - 1},
        1: {-1: gy > 0, 1: gy < NY - 1},
        2: {-1: gz > 0, 1: gz < NZ - 1},
    }
    core = lax.rem(gz, 2)
    started, taken = [], {}

    def exists(o, axes=(0, 1, 2)):
        cond = None
        for axis in axes:
            if o[axis]:
                cond = here[axis][o[axis]] if cond is None else cond & here[axis][o[axis]]
        return cond

    def keep(x, *o, axes=(0, 1, 2)):
        cond = exists(o, axes)
        return x if cond is None else jnp.where(cond, x, 0.0)

    def when(cond, act):
        if cond is None:
            act()
        else:
            pl.when(cond)(act)

    def target(o):
        return (lax.rem(gx + o[0] + NX, NX), lax.rem(gy + o[1] + NY, NY), lax.rem(gz + o[2] + NZ, NZ))

    def send(src, dst, group, o, axes=(0, 1, 2), to=None):
        at = taken.setdefault(group, len(taken))
        copy = pltpu.make_async_remote_copy(
            src_ref=src, dst_ref=dst, send_sem=s["ss"].at[at], recv_sem=s["rs"].at[at],
            device_id=target(o) if to is None else to, device_id_type=MESH,
        )
        out = exists(o, axes)
        when(out, copy.start)
        return group, copy, out, exists(tuple(-d for d in o), axes), int(np.prod(src.shape)) // 1024

    def grouped(copies):
        groups = {}
        for group, copy, out, back, tiles in copies:
            groups.setdefault(group, []).append((copy, out, back, tiles))
        waits = []
        for group, members in groups.items():
            copy, out, back, tiles = members[0]
            if len(members) > 1:
                at, part = taken[group], s["W"].at[pl.ds(0, sum(m[3] for m in members))]
                copy = pltpu.make_async_remote_copy(
                    src_ref=part, dst_ref=part, send_sem=s["ss"].at[at], recv_sem=s["rs"].at[at],
                    device_id=target((0, 0, 1)), device_id_type=MESH,
                )
            started.append((copy, out))
            waits.append((copy, back))
        return waits

    def edges(o):
        axis = next(i for i in range(3) if o[i])
        return jnp.logical_not(here[axis][o[axis]]), s["wrap"], axis

    def tell_edges():
        for o in SIX:
            cond, sem, axis = edges(o)
            when(cond, lambda: pl.semaphore_signal(
                sem.at[axis], inc=1, device_id=target(o), device_id_type=MESH))

    def hear_edges():
        for o in SIX:
            cond, sem, axis = edges(o)
            when(cond, lambda: pl.semaphore_wait(sem.at[axis], 1))

    def arrive(copies):
        for copy, cond in copies:
            when(cond, copy.wait_recv)

    barrier = pltpu.get_barrier_semaphore()
    for o in SIX:
        pl.semaphore_signal(barrier, inc=1, device_id=target(o), device_id_type=MESH)
    main = (pl.ds(1, 16), pl.ds(8, 32))
    loads = [
        pltpu.make_async_copy(c_hbm, s["C0"].at[main], s["hs"].at[0]),
        pltpu.make_async_copy(v_hbm, s["V0"].at[main], s["hs"].at[1]),
        pltpu.make_async_copy(g_hbm, s["GV"], s["hs"].at[2]),
    ]
    for load in loads:
        load.start()

    def pack_fine(plane, k, p, acc):
        s["YB"][0, k, p] = plane[0:1]
        s["YB"][1, k, p] = plane[31:32]
        at = lane((32, 128))
        mine = (at == (2 * p) % 128) | (at == (2 * p - 1) % 128)
        return jnp.where(mine, roll(plane, 2 * p), acc)

    def send_fine(names, k):
        out = []
        yb, rx, ry, rz, pz = s["YB"], s["RX"], s["RY"], s["RZ"], s["PZ"]
        ks = pl.ds(k, len(names))
        out.append(send(yb.at[1, ks], ry.at[0, ks], (k, 0), (0, 1, 0)))
        out.append(send(yb.at[0, ks], ry.at[1, ks], (k, 1), (0, -1, 0)))
        for i, name in enumerate(names):
            low, high = s[name].at[1, pl.ds(8, 32)], s[name].at[16, pl.ds(8, 32)]
            out.append(send(high, rx.at[k + i, 0], (k, 2), (1, 0, 0)))
            out.append(send(low, rx.at[k + i, 1], (k, 3), (-1, 0, 0)))
        out.append(send(pz.at[ks], rz.at[0, ks], (k, 4), (0, 0, 1)))
        out.append(send(pz.at[ks], rz.at[1, ks], (k, 5), (0, 0, -1)))
        return grouped(out)

    def take_fine(name, k):
        v = s[name]
        v[0, 8:40, :] = keep(s["RX"][k, 0], -1, 0, 0)
        v[17, 8:40, :] = keep(s["RX"][k, 1], 1, 0, 0)
        v[1:17, 7:8, :] = keep(s["RY"][0, k], 0, -1, 0)
        v[1:17, 40:41, :] = keep(s["RY"][1, k], 0, 1, 0)
        odd = lane((32, 128)) % 2 == 1
        right, left = keep(s["RZ"][1, k], 0, 0, 1), keep(s["RZ"][0, k], 0, 0, -1)
        s["MZ"][k] = jnp.where(odd, roll(right, -1), roll(left, 1))

    def fine_z(k, extra=None):
        def get(p, v):
            at = lane((32, 128))
            edge = roll(s["MZ"][k], -2 * p)
            if extra is not None:
                edge = edge + extra(p)
            return jnp.where(at == 0, edge, roll(v, 1)), jnp.where(at == 127, edge, roll(v, -1))

        return get

    def plain_z(p, v):
        return roll(v, 1), roll(v, -1)

    def closed_z(p, v):
        at = lane(v.shape)
        return jnp.where(at == 0, 0.0, roll(v, 1)), jnp.where(at == 127, 0.0, roll(v, -1))

    def weights(l, n, rows, scale, zs):
        c, wx, wy = s["C" + l], s["WX" + l], s["WY" + l]
        h = F32(0.5 * scale)
        for p in range(n + 1):
            wx[p] = h * (c[p, 8 : 8 + rows, :] + c[p + 1, 8 : 8 + rows, :])
        for p in range(n):
            wy[p] = h * (c[p + 1, 8 : 16 + rows, :] + c[p + 1, 7 : 15 + rows, :])
            mid = c[p + 1, 8 : 8 + rows, :]
            zm, zp = zs(p, mid)
            wzm, wzp = h * (mid + zm), h * (mid + zp)
            d = wx[p] + wx[p + 1] + wy[p, 0:rows] + wy[p, 1 : rows + 1] + wzm + wzp
            s["WZM" + l][p], s["WZP" + l][p], s["D" + l][p] = wzm, wzp, d
            s["SD" + l][p] = jnp.where(mid > 0, F32(OMEGA) / d, 0.0)

    def gathered(l, v, p, rows, right, zs):
        wx, wy = s["WX" + l], s["WY" + l]
        mid = v[p + 1, 8 : 8 + rows, :]
        zm, zp = zs(p, mid)
        total = right + wx[p] * v[p, 8 : 8 + rows, :] + wx[p + 1] * v[p + 2, 8 : 8 + rows, :]
        total = total + wy[p, 0:rows] * v[p + 1, 7 : 7 + rows, :]
        total = total + wy[p, 1 : rows + 1] * v[p + 1, 9 : 9 + rows, :]
        total = total + s["WZM" + l][p] * zm + s["WZP" + l][p] * zp
        return mid, total

    def swept(l, v, p, rows, right, zs):
        mid, total = gathered(l, v, p, rows, right, zs)
        return mid * F32(1.0 - OMEGA) + s["SD" + l][p] * total

    def residual(l, v, p, rows, right, zs):
        mid, total = gathered(l, v, p, rows, right, zs)
        return total - s["D" + l][p] * mid

    to_one = picks(lambda r, c: r // 2 + 32 == c, value=0.125)
    to_two = [
        picks(lambda r, c, p=p: (c // 32 == p) & (r // 2 == c % 32 + 16), value=0.125) for p in range(4)
    ]
    to_three = [
        picks(lambda r, c, q=q: (c // 16 == 2 * q + core) & (r // 2 == c % 16 + 16), value=0.125)
        for q in range(4)
    ]

    def restrict_fine(plane, k):
        rs = s["RS0"]
        for q in range(8):
            rs[q] = plane(2 * q) + plane(2 * q + 1)
        half = rs[:, pl.ds(0, 16, stride=2), :] + rs[:, pl.ds(1, 16, stride=2), :]
        block = mm(half.reshape(128, 128), to_one).reshape(8, 16, 128)
        s["B1" + k][...] = block
        at = lane((16, 128))
        acc = jnp.zeros((16, 128), F32)
        for p in range(8):
            acc = jnp.where((at >= 16 * p) & (at < 16 * p + 8), roll(block[p], 16 * p - 32), acc)
            acc = jnp.where((at >= 16 * p + 8) & (at < 16 * p + 16), roll(block[p], 16 * p + 8 - 88), acc)
        s["PZ1" + k][...] = acc

    def restrict_one(plane, first, k):
        rs = s["RS1"]
        rows = 24 if first == 4 else 16
        for q in range(4):
            rs[q, 0:rows] = plane(2 * q) + plane(2 * q + 1)
        half = rs[:, pl.ds(first, 8, stride=2), :] + rs[:, pl.ds(first + 1, 8, stride=2), :]
        s["PB2" + k][...] = sum(mm(half[p], to_two[p]) for p in range(4))

    def restrict_two(plane, k):
        rs, qs = s["RS2"], s["QS"]
        for q in range(8):
            rs[q] = plane(2 * q) + plane(2 * q + 1)
        half = rs[:, pl.ds(0, 4, stride=2), :] + rs[:, pl.ds(1, 4, stride=2), :]
        for q in range(4):
            qs[q, 0:4] = half[2 * q]
            qs[q, 4:8] = half[2 * q + 1]
        s["PB3" + k][...] = sum(mm(qs[q], to_three[q]) for q in range(4))

    def send_one(k, h, axes=(0, 1, 2)):
        out = []
        b, pz = s["B1" + k], s["PZ1" + k]
        for i, (dx, dy, dz) in enumerate(AROUND):
            if dz:
                src, dst = pz, s["RZ1" + k].at[side(-dz), 1 - dx, 1 - dy]
            else:
                xs = pl.ds(8 - h, h) if dx > 0 else pl.ds(0, h)
                ys = pl.ds(8, 8) if dy > 0 else pl.ds(0, 8)
                if dx and dy:
                    src, dst = b.at[xs, ys], s["RE1" + k].at[side(-dx), side(-dy)]
                elif dx:
                    src, dst = b.at[xs], s["RX1" + k].at[side(-dx)]
                else:
                    src, dst = b.at[:, ys], s["RY1" + k].at[side(-dy)]
            out.append(send(src, dst, ("one", k, i if axes else 0), (dx, dy, dz), axes))
        return grouped(out)

    def take_one(e, k, h, copies):
        arrive(copies)
        b, rx, ry, re, rz, zs = (s[n + k] for n in ("B1", "RX1", "RY1", "RE1", "RZ1", "ZS"))
        first = lane((16, 128)) % 16 >= 8

        def beside(dx, dy):
            left = keep(rz[0, 1 + dx, 1 + dy], dx, dy, -1)
            right = roll(keep(rz[1, 1 + dx, 1 + dy], dx, dy, 1), 80)
            return jnp.where(first, left, right)

        for dx in (-1, 0, 1):
            zs[1 + dx, 12:28] = beside(dx, 0)
            zs[1 + dx, 12 - h : 12] = beside(dx, -1)[16 - h : 16]
            zs[1 + dx, 28 : 28 + h] = beside(dx, 1)[0:h]
            count, base, start = (8, 5, 0) if dx == 0 else ((h, 5 - h, 8 - h) if dx < 0 else (h, 13, 0))
            planes = pl.ds(base, count)
            if dx == 0:
                e[planes, 12:28, :] = b[...]
                e[planes, 12 - h : 12, :] = keep(ry[0, :, 8 - h : 8, :], 0, -1, 0)
                e[planes, 28 : 28 + h, :] = keep(ry[1, :, 0:h, :], 0, 1, 0)
            else:
                e[planes, 12:28, :] = keep(rx[side(dx)], dx, 0, 0)
                e[planes, 12 - h : 12, :] = keep(re[side(dx), 0, :, 8 - h : 8, :], dx, -1, 0)
                e[planes, 28 : 28 + h, :] = keep(re[side(dx), 1, :, 0:h, :], dx, 1, 0)
            lo, hi = (8, 32) if h == 4 else (0, 40)
            at = lane((hi - lo, 128))
            halo = ((at >= 24) & (at < 32)) | ((at >= 96) & (at < 104))
            for i in range(count):
                moved = roll(zs[1 + dx, lo:hi], 16 - 16 * (start + i))
                e[base + i, lo:hi, :] = jnp.where(halo, moved, e[base + i, lo:hi, :])

    def send_two(k, axes=(1, 2)):
        out = []
        for i, (a, dy, dz) in enumerate(WIDE):
            dst = s["S2" + k].at[gx, 1 - dy, 1 - dz]
            out.append(send(s["PB2" + k], dst, ("two", k, (dy, dz) if axes else 0), (a, dy, dz), axes))
        s["S2" + k][gx, 1, 1] = s["PB2" + k][...]
        return grouped(out)

    def take_two(e, k, copies):
        arrive(copies)
        at = lane((8, 128)) // 32
        for x in range(NX):
            for dy in (-1, 0, 1):
                blocks = [keep(s["S2" + k][x, 1 + dy, 1 + dz], 0, dy, dz) for dz in (-1, 0, 1)]
                for p in range(4):
                    val = jnp.zeros((8, 128), F32)
                    for z in range(3):
                        val = jnp.where(at == z, roll(blocks[z], 32 * (z - p)), val)
                    e[1 + 4 * x + p, 16 + 8 * dy : 24 + 8 * dy, :] = val

    def send_core(k):
        to = (gx, gy, gz + 1 - 2 * core)
        return grouped([send(s["PB3" + k], s["S3" + k], ("core", k), (0, 0, 0), to=to)])

    def send_chips(k, copies):
        arrive(copies)
        s["YS" + k][...] = s["PB3" + k][...] + s["S3" + k][...]
        out = []
        for i, o in enumerate(CHIPS):
            dst = s["S4" + k].at[gy, gz // 2]
            out.append(send(s["YS" + k], dst, ("chips", k), o, ()))
        s["S4" + k][gy, gz // 2] = s["YS" + k][...]
        return grouped(out)

    def take_coarse(dst, base, row, k, copies):
        arrive(copies)
        at = lane((8, 128)) // 32
        for g in range(NY):
            for q in range(4):
                val = jnp.zeros((8, 128), F32)
                for j in range(NZ // 2):
                    val = jnp.where(at == j, roll(s["S4" + k][g, j], 32 * (j - q)), val)
                rows = slice(row + 4 * g, row + 4 * g + 4)
                dst[base + 2 * q, rows, :] = val[0:4]
                dst[base + 2 * q + 1, rows, :] = val[4:8]

    for k, name in ((0, "C0"), (1, "V0")):
        loads[k].wait()
        acc = jnp.zeros((32, 128), F32)
        for p in range(16):
            acc = pack_fine(s[name][p + 1, 8:40, :], k, p, acc)
        s["PZ"][k] = acc
    pl.semaphore_wait(barrier, len(SIX))

    copies = send_fine(("C0", "V0"), 0)
    tell_edges()
    loads[2].wait()
    g_ref = s["GV"]
    for name in ("C1", "G1", "EA1", "EB1", "C2", "G2", "EA2", "EB2"):
        s[name][...] = jnp.zeros((18, 40, 128), F32)
    for name in ("C3", "KA", "KB"):
        s[name][...] = jnp.zeros((10, 48, 128), F32)
    s["ZSc"][...] = jnp.zeros((3, 40, 128), F32)
    s["U2"][...] = jnp.zeros((20, 24, 128), F32)
    s["R3"][...] = jnp.zeros((8, 16, 128), F32)
    s["G3"][...] = jnp.zeros((10, 8, 4, 128), F32)
    restrict_fine(lambda p: s["C0"][p + 1, 8:40, :], "c")
    restrict_one(lambda p: s["B1c"][p], 0, "c")
    arrive(copies)
    hear_edges()
    take_fine("C0", 0)
    weights("0", 16, 32, 1.0, fine_z(0))
    take_fine("V0", 1)

    def sweep_fine(src, dst, zs, k):
        acc = jnp.zeros((32, 128), F32)
        for p in range(16):
            new = swept("0", s[src], p, 32, g_ref[p], zs)
            s[dst][p + 1, 8:40, :] = new
            acc = pack_fine(new, k, p, acc)
        s["PZ"][k] = acc
        return send_fine((dst,), k)

    copies = sweep_fine("V0", "V1", fine_z(1), 2)
    tell_edges()
    arrive(copies)
    hear_edges()
    take_fine("V1", 2)
    copies = sweep_fine("V1", "X0", fine_z(2), 3)
    tell_edges()
    c_one = send_one("c", 5, ())
    arrive(copies)
    hear_edges()
    take_fine("X0", 3)
    restrict_fine(lambda p: residual("0", s["X0"], p, 32, g_ref[p], fine_z(3)), "g")

    g_one = send_one("g", 4)
    take_one(s["C1"], "c", 5, c_one)
    c_two = send_two("c", ())
    weights("1", 16, 24, 0.25, plain_z)
    take_one(s["G1"], "g", 4, g_one)

    def begin(l):
        for p in range(16):
            s["EA" + l][p + 1, 8:32, :] = s["SD" + l][p] * s["G" + l][p + 1, 8:32, :]

    def sweep(l, src, dst):
        for p in range(16):
            right = s["G" + l][p + 1, 8:32, :]
            s[dst][p + 1, 8:32, :] = swept(l, s[src], p, 24, right, plain_z)

    def left(l, src):
        return lambda p: residual(l, s[src], p, 24, s["G" + l][p + 1, 8:32, :], plain_z)

    begin("1")
    sweep("1", "EA1", "EB1")
    rest = left("1", "EB1")
    restrict_one(lambda p: rest(p + 4), 4, "g")

    g_two = send_two("g")
    take_two(s["C2"], "c", c_two)
    restrict_two(lambda p: s["C2"][p + 1, 16:24, :], "c")
    c_core = send_core("c")
    weights("2", 16, 24, 0.0625, plain_z)
    c_chips = send_chips("c", c_core)
    take_two(s["G2"], "g", g_two)
    begin("2")
    sweep("2", "EA2", "EB2")
    rest2 = left("2", "EB2")
    restrict_two(lambda p: rest2(p)[8:16], "g")

    for i, value in enumerate(constants()[0]):
        s["K"][i] = F32(value)
    g_core = send_core("g")
    g_chips = send_chips("g", g_core)
    take_coarse(s["C3"], 1, 8, "c", c_chips)
    weights("3", 8, 32, 0.015625, closed_z)
    at = lane((32, 128))
    for p in range(8):
        inv = F32(1.0) / s["D3"][p]
        s["SD3"][p] = inv
        s["WXM3"][p] = s["WX3"][p] * inv
        s["WXP3"][p] = s["WX3"][p + 1] * inv
        s["WYM3"][p] = s["WY3"][p, 0:32] * inv
        s["WYP3"][p] = s["WY3"][p, 1:33] * inv
        s["WZM3"][p] = jnp.where(at == 0, 0.0, s["WZM3"][p] * inv)
        s["WZP3"][p] = jnp.where(at == 127, 0.0, s["WZP3"][p] * inv)
    take_coarse(s["T3"], 0, 0, "g", g_chips)
    theta = constants()[1]
    for p in range(8):
        t = s["T3"][p] * s["SD3"][p]
        s["T3"][p] = t
        d = t * F32(1.0 / theta)
        s["ST3"][p] = d
        s["KA"][p + 1, 8:40, :] = d

    def cheb(src, dst, i):
        a, b = s["K"][2 * i], s["K"][2 * i + 1]
        v = s[src]
        for p in range(8):
            e = v[p + 1, 8:40, :]
            r = s["T3"][p] - e + s["WXM3"][p] * v[p, 8:40, :] + s["WXP3"][p] * v[p + 2, 8:40, :]
            r = r + s["WYM3"][p] * v[p + 1, 7:39, :] + s["WYP3"][p] * v[p + 1, 9:41, :]
            r = r + s["WZM3"][p] * roll(e, 1) + s["WZP3"][p] * roll(e, -1)
            d = a * s["ST3"][p] + b * r
            s["ST3"][p] = d
            s[dst][p + 1, 8:40, :] = e + d

    def two(i, carry):
        cheb("KA", "KB", 2 * i)
        cheb("KB", "KA", 2 * i + 1)
        return carry

    lax.fori_loop(0, (CHEB - 1) // 2, two, 0)
    cheb("KA", "KB", CHEB - 2)

    for g in range(NY):
        s["G3"][g + 1] = s["KB"][1:9, 8 + 4 * g : 12 + 4 * g, :]
    for j in range(3):
        s["R3"][:, 4 * j : 4 * j + 4, :] = s["G3"][gy + j]
    from_three = picks(lambda r, c: (r == 16 * gz - 16 + c // 2) & (c < 96))
    s["T32"][...] = mm(s["R3"][...].reshape(128, 128), from_three).reshape(8, 16, 128)
    for o in (0, 1):
        s["D32"][:, pl.ds(o, 12, stride=2), :] = s["T32"][:, 0:12, :]
    for p in range(16):
        s["EA2"][p + 1, 8:32, :] = s["EB2"][p + 1, 8:32, :] + s["D32"][p // 2]
    sweep("2", "EA2", "EB2")
    for p in range(16):
        right = s["G2"][p + 1, 8:32, :]
        s["U2"][p + 2] = swept("2", s["EB2"], p, 24, right, plain_z)

    from_two = picks(lambda r, c: (r == 16 + c // 2) & (c >= 24) & (c < 104))
    part = s["U2"][pl.ds(4 * gx, 8)]
    s["T21"][...] = mm(part.reshape(192, 128), from_two).reshape(8, 24, 128)
    for o in (0, 1):
        s["D21"][:, pl.ds(o, 12, stride=2), :] = s["T21"][:, 6:18, :]
    for p in range(16):
        s["EA1"][p + 1, 8:32, :] = s["EB1"][p + 1, 8:32, :] + s["D21"][p // 2]
    sweep("1", "EA1", "EB1")
    sweep("1", "EB1", "EA1")

    from_one = picks(
        lambda r, c: ((c < 128) & (r == 32 + c // 2)) | ((c == 128) & (r == 31)) | ((c == 255) & (r == 96)), 256
    )
    wide = mm(s["EA1"][4:14, 8:32, :].reshape(240, 128), from_one)
    s["TA"][...] = wide[:, 0:128].reshape(10, 24, 128)
    s["TB"][...] = wide[:, 128:256].reshape(10, 24, 128)
    for o in (0, 1):
        s["DA"][:, pl.ds(8 + o, 16, stride=2), :] = s["TA"][:, 4:20, :]
        s["DB"][:, pl.ds(o, 16, stride=2), :] = s["TB"][:, 4:20, :]
    for i in range(18):
        j = (i + 1) // 2
        s["VP"][i, 8:40, :] = s["X0"][i, 8:40, :] + s["DA"][j, 8:40, :]
        if 0 < i < 17:
            s["VP"][i, 7:8, :] = s["X0"][i, 7:8, :] + s["TA"][j, 3:4, :]
            s["VP"][i, 40:41, :] = s["X0"][i, 40:41, :] + s["TA"][j, 20:21, :]
    copies = sweep_fine("VP", "VQ", fine_z(3, lambda p: s["DB"][(p + 2) // 2]), 4)
    arrive(copies)
    take_fine("VQ", 4)
    stores = []
    for p in range(16):
        s["OV"][p] = swept("0", s["VQ"], p, 32, g_ref[p], fine_z(4))
        if p % 4 == 3:
            part = pl.ds(p - 3, 4)
            stores.append(pltpu.make_async_copy(s["OV"].at[part], o_ref.at[part], s["hs"].at[3 + p // 4]))
            stores[-1].start()
    for copy, cond in started:
        when(cond, copy.wait_send)
    for copy in stores:
        copy.wait()


def on_device(right_side, coefficient, guess):
    whole = pl.BlockSpec(memory_space=pl.ANY)
    return pl.pallas_call(
        kernel,
        out_shape=jax.ShapeDtypeStruct((16, 32, 128), F32),
        in_specs=[whole, whole, whole],
        out_specs=whole,
        scratch_shapes=[build_scratch()],
        compiler_params=pltpu.CompilerParams(
            collective_id=0, has_side_effects=True, vmem_limit_bytes=56 * 2**20
        ),
    )(right_side, coefficient, guess)


def solution(mesh):
    spec = P("gx", "gy", "gz")
    return jax.shard_map(on_device, mesh=mesh, in_specs=(spec, spec, spec), out_specs=spec, check_vma=False)
```

```python
import itertools

import jax
import jax.numpy as jnp
import numpy as np
from jax import lax
from jax.experimental import pallas as pl
from jax.experimental.pallas import tpu as pltpu
from jax.sharding import PartitionSpec as P

CHEB = 20
OMEGA = 2.0 / 3.0
CHEB_LOW = 0.1
CHEB_HIGH = 2.0
MESH = pl.DeviceIdType.MESH
F32 = jnp.float32
NX, NY, NZ = 4, 8, 8
SIX = ((1, 0, 0), (-1, 0, 0), (0, 1, 0), (0, -1, 0), (0, 0, 1), (0, 0, -1))
AROUND = sorted(
    (o for o in itertools.product((-1, 0, 1), repeat=3) if o != (0, 0, 0)),
    key=lambda o: -(abs(o[0]) + abs(o[1]) + abs(o[2])),
)
WIDE = sorted(
    (o for o in itertools.product(range(NX), (-1, 0, 1), (-1, 0, 1)) if o != (0, 0, 0)),
    key=lambda o: -((o[0] != 0) + (o[0] == 2) + abs(o[1]) + abs(o[2])),
)
CHIPS = sorted(
    (o for o in itertools.product((0,), range(NY), range(0, NZ, 2)) if o != (0, 0, 0)),
    key=lambda o: -(min(o[1], NY - o[1]) + min(o[2], NZ - o[2]) // 2),
)

def side(d):
    return 0 if d < 0 else 1


def constants():
    theta, delta = 0.5 * (CHEB_HIGH + CHEB_LOW), 0.5 * (CHEB_HIGH - CHEB_LOW)
    sigma = theta / delta
    rho, out = np.float32(1.0 / sigma), []
    for _ in range(CHEB - 1):
        rho_next = np.float32(1.0 / (2.0 * sigma - rho))
        out += [np.float32(rho_next * rho), np.float32(2.0 * rho_next / delta)]
        rho = rho_next
    return np.array(out, np.float32), theta


def lane(shape):
    return lax.broadcasted_iota(jnp.int32, shape, len(shape) - 1)


def roll(x, by):
    return pltpu.roll(x, by % 128, x.ndim - 1)


def mm(x, m):
    rows = x.shape[0]
    high = x.astype(jnp.bfloat16)
    rest = x - high.astype(F32)
    mid = rest.astype(jnp.bfloat16)
    low = (rest - mid.astype(F32)).astype(jnp.bfloat16)
    terms = jnp.concatenate([high, mid, low], axis=0)
    out = lax.dot_general(terms, m, (((1,), (0,)), ((), ())), preferred_element_type=F32)
    return out[0:rows] + out[rows : 2 * rows] + out[2 * rows :]


def picks(condition, width=128, value=1.0):
    row = lax.broadcasted_iota(jnp.int32, (128, width), 0)
    col = lax.broadcasted_iota(jnp.int32, (128, width), 1)
    return jnp.where(condition(row, col), F32(value), F32(0.0)).astype(jnp.bfloat16)


def vm(*shape):
    return pltpu.VMEM(shape, F32)


def dma(*shape):
    return pltpu.SemaphoreType.DMA(shape)


def build_scratch():
    s = {}
    for name in ("C0", "V0", "V1", "X0", "VP", "VQ"):
        s[name] = vm(18, 48, 128)
    s.update(WX0=vm(17, 32, 128), WY0=vm(16, 40, 128))
    for name in ("WZM0", "WZP0", "D0", "SD0"):
        s[name] = vm(16, 32, 128)
    s.update(
        YB=vm(2, 5, 16, 1, 128), PZ=vm(5, 32, 128),
        RX=vm(5, 2, 32, 128), RY=vm(2, 5, 16, 1, 128), RZ=vm(2, 5, 32, 128), MZ=vm(5, 32, 128),
        ss=dma(42), rs=dma(42), W=vm(92, 8, 128), hs=dma(8), GV=vm(16, 32, 128), OV=vm(16, 32, 128),
    )
    s.update(RS0=vm(8, 32, 128), RS1=vm(4, 24, 128), RS2=vm(8, 8, 128), QS=vm(4, 8, 128))
    for k, h in (("c", 5), ("g", 4)):
        s["B1" + k] = vm(8, 16, 128)
        s["PZ1" + k] = vm(16, 128)
        s["RX1" + k] = vm(2, h, 16, 128)
        s["RY1" + k] = vm(2, 8, 8, 128)
        s["RE1" + k] = vm(2, 2, h, 8, 128)
        s["RZ1" + k] = vm(2, 3, 3, 16, 128)
        s["ZS" + k] = vm(3, 40, 128)
        s["PB2" + k] = vm(8, 128)
        s["S2" + k] = vm(NX, 3, 3, 8, 128)
        s["PB3" + k] = vm(8, 128)
        s["S3" + k] = vm(8, 128)
        s["YS" + k] = vm(8, 128)
        s["S4" + k] = vm(NY, NZ // 2, 8, 128)
    for l in ("1", "2"):
        for name in ("C", "G", "EA", "EB"):
            s[name + l] = vm(18, 40, 128)
        s.update({"WX" + l: vm(17, 24, 128), "WY" + l: vm(16, 32, 128)})
        for name in ("WZM", "WZP", "D", "SD"):
            s[name + l] = vm(16, 24, 128)
    s["wrap"] = pltpu.SemaphoreType.REGULAR((3,))
    s["K"] = pltpu.SMEM((2 * (CHEB - 1),), F32)
    s.update(U2=vm(20, 24, 128), T21=vm(8, 24, 128), D21=vm(8, 24, 128))
    s.update(TA=vm(10, 24, 128), TB=vm(10, 24, 128), DA=vm(10, 48, 128), DB=vm(10, 32, 128))
    s.update(C3=vm(10, 48, 128), T3=vm(8, 32, 128), KA=vm(10, 48, 128), KB=vm(10, 48, 128), ST3=vm(8, 32, 128))
    s.update(WX3=vm(9, 32, 128), WY3=vm(8, 40, 128))
    for name in ("WXM3", "WXP3", "WYM3", "WYP3", "WZM3", "WZP3", "D3", "SD3"):
        s[name] = vm(8, 32, 128)
    s.update(G3=vm(10, 8, 4, 128), R3=vm(8, 16, 128), T32=vm(8, 16, 128), D32=vm(8, 24, 128))
    return s


def kernel(g_hbm, c_hbm, v_hbm, o_ref, s):
    gx, gy, gz = (lax.axis_index(a) for a in ("gx", "gy", "gz"))
    here = {
        0: {-1: gx > 0, 1: gx < NX - 1},
        1: {-1: gy > 0, 1: gy < NY - 1},
        2: {-1: gz > 0, 1: gz < NZ - 1},
    }
    core = lax.rem(gz, 2)
    started, taken = [], {}

    def exists(o, axes=(0, 1, 2)):
        cond = None
        for axis in axes:
            if o[axis]:
                cond = here[axis][o[axis]] if cond is None else cond & here[axis][o[axis]]
        return cond

    def keep(x, *o, axes=(0, 1, 2)):
        cond = exists(o, axes)
        return x if cond is None else jnp.where(cond, x, 0.0)

    def when(cond, act):
        if cond is None:
            act()
        else:
            pl.when(cond)(act)

    def target(o):
        return (lax.rem(gx + o[0] + NX, NX), lax.rem(gy + o[1] + NY, NY), lax.rem(gz + o[2] + NZ, NZ))

    def send(src, dst, group, o, axes=(0, 1, 2), to=None):
        at = taken.setdefault(group, len(taken))
        copy = pltpu.make_async_remote_copy(
            src_ref=src, dst_ref=dst, send_sem=s["ss"].at[at], recv_sem=s["rs"].at[at],
            device_id=target(o) if to is None else to, device_id_type=MESH,
        )
        out = exists(o, axes)
        when(out, copy.start)
        return group, copy, out, exists(tuple(-d for d in o), axes), int(np.prod(src.shape)) // 1024

    def grouped(copies):
        groups = {}
        for group, copy, out, back, tiles in copies:
            groups.setdefault(group, []).append((copy, out, back, tiles))
        waits = []
        for group, members in groups.items():
            copy, out, back, tiles = members[0]
            if len(members) > 1:
                at, part = taken[group], s["W"].at[pl.ds(0, sum(m[3] for m in members))]
                copy = pltpu.make_async_remote_copy(
                    src_ref=part, dst_ref=part, send_sem=s["ss"].at[at], recv_sem=s["rs"].at[at],
                    device_id=target((0, 0, 1)), device_id_type=MESH,
                )
            started.append((copy, out))
            waits.append((copy, back))
        return waits

    def edges(o):
        axis = next(i for i in range(3) if o[i])
        return jnp.logical_not(here[axis][o[axis]]), s["wrap"], axis

    def tell_edges():
        for o in SIX:
            cond, sem, axis = edges(o)
            when(cond, lambda: pl.semaphore_signal(
                sem.at[axis], inc=1, device_id=target(o), device_id_type=MESH))

    def hear_edges():
        for o in SIX:
            cond, sem, axis = edges(o)
            when(cond, lambda: pl.semaphore_wait(sem.at[axis], 1))

    def arrive(copies):
        for copy, cond in copies:
            when(cond, copy.wait_recv)

    barrier = pltpu.get_barrier_semaphore()
    for o in SIX:
        pl.semaphore_signal(barrier, inc=1, device_id=target(o), device_id_type=MESH)
    main = (pl.ds(1, 16), pl.ds(8, 32))
    loads = [
        pltpu.make_async_copy(c_hbm, s["C0"].at[main], s["hs"].at[0]),
        pltpu.make_async_copy(v_hbm, s["V0"].at[main], s["hs"].at[1]),
        pltpu.make_async_copy(g_hbm, s["GV"], s["hs"].at[2]),
    ]
    for load in loads:
        load.start()

    def pack_fine(plane, k, p, acc):
        s["YB"][0, k, p] = plane[0:1]
        s["YB"][1, k, p] = plane[31:32]
        at = lane((32, 128))
        mine = (at == (2 * p) % 128) | (at == (2 * p - 1) % 128)
        return jnp.where(mine, roll(plane, 2 * p), acc)

    def send_fine(names, k):
        out = []
        yb, rx, ry, rz, pz = s["YB"], s["RX"], s["RY"], s["RZ"], s["PZ"]
        ks = pl.ds(k, len(names))
        out.append(send(yb.at[1, ks], ry.at[0, ks], (k, 0), (0, 1, 0)))
        out.append(send(yb.at[0, ks], ry.at[1, ks], (k, 1), (0, -1, 0)))
        for i, name in enumerate(names):
            low, high = s[name].at[1, pl.ds(8, 32)], s[name].at[16, pl.ds(8, 32)]
            out.append(send(high, rx.at[k + i, 0], (k, 2), (1, 0, 0)))
            out.append(send(low, rx.at[k + i, 1], (k, 3), (-1, 0, 0)))
        out.append(send(pz.at[ks], rz.at[0, ks], (k, 4), (0, 0, 1)))
        out.append(send(pz.at[ks], rz.at[1, ks], (k, 5), (0, 0, -1)))
        return grouped(out)

    def take_fine(name, k):
        v = s[name]
        v[0, 8:40, :] = keep(s["RX"][k, 0], -1, 0, 0)
        v[17, 8:40, :] = keep(s["RX"][k, 1], 1, 0, 0)
        v[1:17, 7:8, :] = keep(s["RY"][0, k], 0, -1, 0)
        v[1:17, 40:41, :] = keep(s["RY"][1, k], 0, 1, 0)
        odd = lane((32, 128)) % 2 == 1
        right, left = keep(s["RZ"][1, k], 0, 0, 1), keep(s["RZ"][0, k], 0, 0, -1)
        s["MZ"][k] = jnp.where(odd, roll(right, -1), roll(left, 1))

    def fine_z(k, extra=None):
        def get(p, v):
            at = lane((32, 128))
            edge = roll(s["MZ"][k], -2 * p)
            if extra is not None:
                edge = edge + extra(p)
            return jnp.where(at == 0, edge, roll(v, 1)), jnp.where(at == 127, edge, roll(v, -1))

        return get

    def plain_z(p, v):
        return roll(v, 1), roll(v, -1)

    def closed_z(p, v):
        at = lane(v.shape)
        return jnp.where(at == 0, 0.0, roll(v, 1)), jnp.where(at == 127, 0.0, roll(v, -1))

    def weights(l, n, rows, scale, zs):
        c, wx, wy = s["C" + l], s["WX" + l], s["WY" + l]
        h = F32(0.5 * scale)
        for p in range(n + 1):
            wx[p] = h * (c[p, 8 : 8 + rows, :] + c[p + 1, 8 : 8 + rows, :])
        for p in range(n):
            wy[p] = h * (c[p + 1, 8 : 16 + rows, :] + c[p + 1, 7 : 15 + rows, :])
            mid = c[p + 1, 8 : 8 + rows, :]
            zm, zp = zs(p, mid)
            wzm, wzp = h * (mid + zm), h * (mid + zp)
            d = wx[p] + wx[p + 1] + wy[p, 0:rows] + wy[p, 1 : rows + 1] + wzm + wzp
            s["WZM" + l][p], s["WZP" + l][p], s["D" + l][p] = wzm, wzp, d
            s["SD" + l][p] = jnp.where(mid > 0, F32(OMEGA) / d, 0.0)

    def gathered(l, v, p, rows, right, zs, skip=0):
        wx, wy = s["WX" + l], s["WY" + l]
        lo, hi, up, here_ = 8 + skip, 8 + skip + rows, slice(skip + 1, skip + rows + 1), slice(skip, skip + rows)
        mid = v[p + 1, lo:hi, :]
        zm, zp = zs(p, mid)
        total = right + wx[p, here_] * v[p, lo:hi, :] + wx[p + 1, here_] * v[p + 2, lo:hi, :]
        total = total + wy[p, here_] * v[p + 1, lo - 1 : hi - 1, :]
        total = total + wy[p, up] * v[p + 1, lo + 1 : hi + 1, :]
        total = total + s["WZM" + l][p, here_] * zm + s["WZP" + l][p, here_] * zp
        return mid, total

    def swept(l, v, p, rows, right, zs):
        mid, total = gathered(l, v, p, rows, right, zs)
        return mid * F32(1.0 - OMEGA) + s["SD" + l][p] * total

    def residual(l, v, p, rows, right, zs, skip=0):
        mid, total = gathered(l, v, p, rows, right, zs, skip)
        return total - s["D" + l][p, skip : skip + rows] * mid

    to_one = picks(lambda r, c: r // 2 + 32 == c, value=0.125)
    to_two = picks(lambda r, c: (c < 32) & (r // 2 == c + 16), value=0.125)
    to_three = picks(lambda r, c: (c // 16 == core) & (r // 2 == c % 16 + 16), value=0.125)

    def side_by_side(x, m):
        out = mm(x.reshape(32, 128), m)
        return out[0:8] + roll(out[8:16], 32) + roll(out[16:24], 64) + roll(out[24:32], 96)

    def restrict_fine(plane, k):
        rs = s["RS0"]
        for q in range(8):
            rs[q] = plane(2 * q) + plane(2 * q + 1)
        half = rs[:, pl.ds(0, 16, stride=2), :] + rs[:, pl.ds(1, 16, stride=2), :]
        block = mm(half.reshape(128, 128), to_one).reshape(8, 16, 128)
        s["B1" + k][...] = block
        at = lane((16, 128))
        acc = jnp.zeros((16, 128), F32)
        for p in range(8):
            acc = jnp.where((at >= 16 * p) & (at < 16 * p + 8), roll(block[p], 16 * p - 32), acc)
            acc = jnp.where((at >= 16 * p + 8) & (at < 16 * p + 16), roll(block[p], 16 * p + 8 - 88), acc)
        s["PZ1" + k][...] = acc

    def restrict_one(plane, first, k):
        rs = s["RS1"]
        rows = 24 if first == 4 else 16
        for q in range(4):
            rs[q, 0:rows] = plane(2 * q) + plane(2 * q + 1)
        half = rs[:, pl.ds(first, 8, stride=2), :] + rs[:, pl.ds(first + 1, 8, stride=2), :]
        s["PB2" + k][...] = side_by_side(half, to_two)

    def restrict_two(plane, k):
        rs, qs = s["RS2"], s["QS"]
        for q in range(8):
            rs[q] = plane(2 * q) + plane(2 * q + 1)
        half = rs[:, pl.ds(0, 4, stride=2), :] + rs[:, pl.ds(1, 4, stride=2), :]
        for q in range(4):
            qs[q, 0:4] = half[2 * q]
            qs[q, 4:8] = half[2 * q + 1]
        s["PB3" + k][...] = side_by_side(qs[...], to_three)

    def send_one(k, h, axes=(0, 1)):
        out = []
        b, pz = s["B1" + k], s["PZ1" + k]
        for i, (dx, dy, dz) in enumerate(AROUND):
            if dz:
                src, dst = pz, s["RZ1" + k].at[side(-dz), 1 - dx, 1 - dy]
            else:
                xs = pl.ds(8 - h, h) if dx > 0 else pl.ds(0, h)
                ys = pl.ds(8, 8) if dy > 0 else pl.ds(0, 8)
                if dx and dy:
                    src, dst = b.at[xs, ys], s["RE1" + k].at[side(-dx), side(-dy)]
                elif dx:
                    src, dst = b.at[xs], s["RX1" + k].at[side(-dx)]
                else:
                    src, dst = b.at[:, ys], s["RY1" + k].at[side(-dy)]
            out.append(send(src, dst, ("one", k, (dx, dy) if axes else 0), (dx, dy, dz), axes))
        return grouped(out)

    def take_one(e, k, h, copies):
        arrive(copies)
        b, rx, ry, re, rz, zs = (s[n + k] for n in ("B1", "RX1", "RY1", "RE1", "RZ1", "ZS"))
        first = lane((16, 128)) % 16 >= 8

        def beside(dx, dy):
            left = keep(rz[0, 1 + dx, 1 + dy], dx, dy, -1)
            right = roll(keep(rz[1, 1 + dx, 1 + dy], dx, dy, 1), 80)
            return jnp.where(first, left, right)

        for dx in (-1, 0, 1):
            zs[1 + dx, 12:28] = beside(dx, 0)
            zs[1 + dx, 12 - h : 12] = beside(dx, -1)[16 - h : 16]
            zs[1 + dx, 28 : 28 + h] = beside(dx, 1)[0:h]
            count, base, start = (8, 5, 0) if dx == 0 else ((h, 5 - h, 8 - h) if dx < 0 else (h, 13, 0))
            planes = pl.ds(base, count)
            if dx == 0:
                e[planes, 12:28, :] = b[...]
                e[planes, 12 - h : 12, :] = keep(ry[0, :, 8 - h : 8, :], 0, -1, 0)
                e[planes, 28 : 28 + h, :] = keep(ry[1, :, 0:h, :], 0, 1, 0)
            else:
                e[planes, 12:28, :] = keep(rx[side(dx)], dx, 0, 0)
                e[planes, 12 - h : 12, :] = keep(re[side(dx), 0, :, 8 - h : 8, :], dx, -1, 0)
                e[planes, 28 : 28 + h, :] = keep(re[side(dx), 1, :, 0:h, :], dx, 1, 0)
            lo, hi = (8, 32) if h == 4 else (0, 40)
            at = lane((hi - lo, 128))
            halo = ((at >= 24) & (at < 32)) | ((at >= 96) & (at < 104))
            for i in range(count):
                moved = roll(zs[1 + dx, lo:hi], 16 - 16 * (start + i))
                e[base + i, lo:hi, :] = jnp.where(halo, moved, e[base + i, lo:hi, :])

    def send_two(k, axes=(1,)):
        out = []
        for i, (a, dy, dz) in enumerate(WIDE):
            dst = s["S2" + k].at[gx, 1 - dy, 1 - dz]
            out.append(send(s["PB2" + k], dst, ("two", k, dy if axes else 0), (a, dy, dz), axes))
        s["S2" + k][gx, 1, 1] = s["PB2" + k][...]
        return grouped(out)

    def take_two(e, k, copies):
        arrive(copies)
        at = lane((8, 128)) // 32
        for x in range(NX):
            for dy in (-1, 0, 1):
                blocks = [keep(s["S2" + k][x, 1 + dy, 1 + dz], 0, dy, dz) for dz in (-1, 0, 1)]
                for p in range(4):
                    val = jnp.zeros((8, 128), F32)
                    for z in range(3):
                        val = jnp.where(at == z, roll(blocks[z], 32 * (z - p)), val)
                    e[1 + 4 * x + p, 16 + 8 * dy : 24 + 8 * dy, :] = val

    def send_core(k):
        to = (gx, gy, gz + 1 - 2 * core)
        return grouped([send(s["PB3" + k], s["S3" + k], ("core", k), (0, 0, 0), to=to)])

    def send_chips(k, copies):
        arrive(copies)
        s["YS" + k][...] = s["PB3" + k][...] + s["S3" + k][...]
        out = []
        for i, o in enumerate(CHIPS):
            dst = s["S4" + k].at[gy, gz // 2]
            out.append(send(s["YS" + k], dst, ("chips", k), o, ()))
        s["S4" + k][gy, gz // 2] = s["YS" + k][...]
        return grouped(out)

    def take_coarse(dst, base, row, k, copies):
        arrive(copies)
        at = lane((8, 128)) // 32
        for g in range(NY):
            for q in range(4):
                val = jnp.zeros((8, 128), F32)
                for j in range(NZ // 2):
                    val = jnp.where(at == j, roll(s["S4" + k][g, j], 32 * (j - q)), val)
                rows = slice(row + 4 * g, row + 4 * g + 4)
                dst[base + 2 * q, rows, :] = val[0:4]
                dst[base + 2 * q + 1, rows, :] = val[4:8]

    for k, name in ((0, "C0"), (1, "V0")):
        loads[k].wait()
        acc = jnp.zeros((32, 128), F32)
        for p in range(16):
            acc = pack_fine(s[name][p + 1, 8:40, :], k, p, acc)
        s["PZ"][k] = acc
    pl.semaphore_wait(barrier, len(SIX))

    copies = send_fine(("C0", "V0"), 0)
    tell_edges()
    loads[2].wait()
    g_ref = s["GV"]
    for name in ("C1", "G1", "EA1", "EB1", "C2", "G2", "EA2", "EB2"):
        s[name][...] = jnp.zeros((18, 40, 128), F32)
    for name in ("C3", "KA", "KB"):
        s[name][...] = jnp.zeros((10, 48, 128), F32)
    s["ZSc"][...] = jnp.zeros((3, 40, 128), F32)
    s["U2"][...] = jnp.zeros((20, 24, 128), F32)
    s["R3"][...] = jnp.zeros((8, 16, 128), F32)
    s["G3"][...] = jnp.zeros((10, 8, 4, 128), F32)
    restrict_fine(lambda p: s["C0"][p + 1, 8:40, :], "c")
    restrict_one(lambda p: s["B1c"][p], 0, "c")
    arrive(copies)
    hear_edges()
    take_fine("C0", 0)
    weights("0", 16, 32, 1.0, fine_z(0))
    take_fine("V0", 1)

    def sweep_fine(src, dst, zs, k):
        acc = jnp.zeros((32, 128), F32)
        for p in range(16):
            new = swept("0", s[src], p, 32, g_ref[p], zs)
            s[dst][p + 1, 8:40, :] = new
            acc = pack_fine(new, k, p, acc)
        s["PZ"][k] = acc
        return send_fine((dst,), k)

    copies = sweep_fine("V0", "V1", fine_z(1), 2)
    tell_edges()
    arrive(copies)
    hear_edges()
    take_fine("V1", 2)
    copies = sweep_fine("V1", "X0", fine_z(2), 3)
    tell_edges()
    c_one = send_one("c", 5, ())
    arrive(copies)
    hear_edges()
    take_fine("X0", 3)
    restrict_fine(lambda p: residual("0", s["X0"], p, 32, g_ref[p], fine_z(3)), "g")

    g_one = send_one("g", 4)
    take_one(s["C1"], "c", 5, c_one)
    c_two = send_two("c", ())
    weights("1", 16, 24, 0.25, plain_z)
    take_one(s["G1"], "g", 4, g_one)

    def begin(l, planes=range(16)):
        for p in planes:
            s["EA" + l][p + 1, 8:32, :] = s["SD" + l][p] * s["G" + l][p + 1, 8:32, :]

    def sweep(l, src, dst, planes=range(16)):
        for p in planes:
            right = s["G" + l][p + 1, 8:32, :]
            s[dst][p + 1, 8:32, :] = swept(l, s[src], p, 24, right, plain_z)

    def left(l, src):
        return lambda p: residual(l, s[src], p, 24, s["G" + l][p + 1, 8:32, :], plain_z)

    begin("1")
    sweep("1", "EA1", "EB1", range(1, 15))
    rest = left("1", "EB1")
    restrict_one(lambda p: rest(p + 4), 4, "g")

    g_two = send_two("g")
    take_two(s["C2"], "c", c_two)
    restrict_two(lambda p: s["C2"][p + 1, 16:24, :], "c")
    c_core = send_core("c")
    weights("2", 16, 24, 0.0625, plain_z)
    c_chips = send_chips("c", c_core)
    take_two(s["G2"], "g", g_two)
    begin("2")
    sweep("2", "EA2", "EB2")
    restrict_two(lambda p: residual("2", s["EB2"], p, 8, s["G2"][p + 1, 16:24, :], plain_z, 8), "g")

    for i, value in enumerate(constants()[0]):
        s["K"][i] = F32(value)
    g_core = send_core("g")
    g_chips = send_chips("g", g_core)
    take_coarse(s["C3"], 1, 8, "c", c_chips)
    weights("3", 8, 32, 0.015625, closed_z)
    at = lane((32, 128))
    for p in range(8):
        inv = F32(1.0) / s["D3"][p]
        s["SD3"][p] = inv
        s["WXM3"][p] = s["WX3"][p] * inv
        s["WXP3"][p] = s["WX3"][p + 1] * inv
        s["WYM3"][p] = s["WY3"][p, 0:32] * inv
        s["WYP3"][p] = s["WY3"][p, 1:33] * inv
        s["WZM3"][p] = jnp.where(at == 0, 0.0, s["WZM3"][p] * inv)
        s["WZP3"][p] = jnp.where(at == 127, 0.0, s["WZP3"][p] * inv)
    take_coarse(s["T3"], 0, 0, "g", g_chips)
    theta = constants()[1]
    for p in range(8):
        t = s["T3"][p] * s["SD3"][p]
        s["T3"][p] = t
        d = t * F32(1.0 / theta)
        s["ST3"][p] = d
        s["KA"][p + 1, 8:40, :] = d

    def cheb(src, dst, i):
        a, b = s["K"][2 * i], s["K"][2 * i + 1]
        v = s[src]
        for p in range(8):
            e = v[p + 1, 8:40, :]
            r = s["T3"][p] - e + s["WXM3"][p] * v[p, 8:40, :] + s["WXP3"][p] * v[p + 2, 8:40, :]
            r = r + s["WYM3"][p] * v[p + 1, 7:39, :] + s["WYP3"][p] * v[p + 1, 9:41, :]
            r = r + s["WZM3"][p] * roll(e, 1) + s["WZP3"][p] * roll(e, -1)
            d = a * s["ST3"][p] + b * r
            s["ST3"][p] = d
            s[dst][p + 1, 8:40, :] = e + d

    def two(i, carry):
        cheb("KA", "KB", 2 * i)
        cheb("KB", "KA", 2 * i + 1)
        return carry

    lax.fori_loop(0, (CHEB - 1) // 2, two, 0)
    cheb("KA", "KB", CHEB - 2)

    for g in range(NY):
        s["G3"][g + 1] = s["KB"][1:9, 8 + 4 * g : 12 + 4 * g, :]
    for j in range(3):
        s["R3"][:, 4 * j : 4 * j + 4, :] = s["G3"][gy + j]
    from_three = picks(lambda r, c: (r == 16 * gz - 16 + c // 2) & (c < 96))
    s["T32"][...] = mm(s["R3"][...].reshape(128, 128), from_three).reshape(8, 16, 128)
    for o in (0, 1):
        s["D32"][:, pl.ds(o, 12, stride=2), :] = s["T32"][:, 0:12, :]
    for p in range(16):
        s["EA2"][p + 1, 8:32, :] = s["EB2"][p + 1, 8:32, :] + s["D32"][p // 2]
    sweep("2", "EA2", "EB2")
    for p in range(16):
        right = s["G2"][p + 1, 8:32, :]
        s["U2"][p + 2] = swept("2", s["EB2"], p, 24, right, plain_z)

    from_two = picks(lambda r, c: (r == 16 + c // 2) & (c >= 24) & (c < 104))
    part = s["U2"][pl.ds(4 * gx, 8)]
    s["T21"][...] = mm(part.reshape(192, 128), from_two).reshape(8, 24, 128)
    for o in (0, 1):
        s["D21"][:, pl.ds(o, 12, stride=2), :] = s["T21"][:, 6:18, :]
    for p in range(1, 15):
        s["EA1"][p + 1, 8:32, :] = s["EB1"][p + 1, 8:32, :] + s["D21"][p // 2]
    sweep("1", "EA1", "EB1", range(2, 14))
    sweep("1", "EB1", "EA1", range(3, 13))

    from_one = picks(
        lambda r, c: ((c < 128) & (r == 32 + c // 2)) | ((c == 128) & (r == 31)) | ((c == 255) & (r == 96)), 256
    )
    wide = mm(s["EA1"][4:14, 8:32, :].reshape(240, 128), from_one)
    s["TA"][...] = wide[:, 0:128].reshape(10, 24, 128)
    s["TB"][...] = wide[:, 128:256].reshape(10, 24, 128)
    for o in (0, 1):
        s["DA"][:, pl.ds(8 + o, 16, stride=2), :] = s["TA"][:, 4:20, :]
        s["DB"][:, pl.ds(o, 16, stride=2), :] = s["TB"][:, 4:20, :]
    for i in range(18):
        j = (i + 1) // 2
        s["VP"][i, 8:40, :] = s["X0"][i, 8:40, :] + s["DA"][j, 8:40, :]
        if 0 < i < 17:
            s["VP"][i, 7:8, :] = s["X0"][i, 7:8, :] + s["TA"][j, 3:4, :]
            s["VP"][i, 40:41, :] = s["X0"][i, 40:41, :] + s["TA"][j, 20:21, :]
    earlier = len(started)
    copies = sweep_fine("VP", "VQ", fine_z(3, lambda p: s["DB"][(p + 2) // 2]), 4)
    for copy, cond in started[:earlier]:
        when(cond, copy.wait_send)
    arrive(copies)
    take_fine("VQ", 4)
    stores = []
    for p in range(16):
        s["OV"][p] = swept("0", s["VQ"], p, 32, g_ref[p], fine_z(4))
        if p % 4 == 3:
            part = pl.ds(p - 3, 4)
            stores.append(pltpu.make_async_copy(s["OV"].at[part], o_ref.at[part], s["hs"].at[3 + p // 4]))
            stores[-1].start()
    for copy, cond in started[earlier:]:
        when(cond, copy.wait_send)
    for copy in stores:
        copy.wait()


def on_device(right_side, coefficient, guess):
    whole = pl.BlockSpec(memory_space=pl.ANY)
    return pl.pallas_call(
        kernel,
        out_shape=jax.ShapeDtypeStruct((16, 32, 128), F32),
        in_specs=[whole, whole, whole],
        out_specs=whole,
        scratch_shapes=[build_scratch()],
        compiler_params=pltpu.CompilerParams(
            collective_id=0, has_side_effects=True, vmem_limit_bytes=56 * 2**20
        ),
    )(right_side, coefficient, guess)


def solution(mesh):
    spec = P("gx", "gy", "gz")
    return jax.shard_map(on_device, mesh=mesh, in_specs=(spec, spec, spec), out_specs=spec, check_vma=False)
```

```python
import itertools

import jax
import jax.numpy as jnp
import numpy as np
from jax import lax
from jax.experimental import pallas as pl
from jax.experimental.pallas import tpu as pltpu
from jax.sharding import PartitionSpec as P

CHEB = 20
OMEGA = 2.0 / 3.0
CHEB_LOW = 0.1
CHEB_HIGH = 2.0
MESH = pl.DeviceIdType.MESH
F32 = jnp.float32
NX, NY, NZ = 4, 8, 8
SIX = ((1, 0, 0), (-1, 0, 0), (0, 1, 0), (0, -1, 0), (0, 0, 1), (0, 0, -1))
AROUND = sorted(
    (o for o in itertools.product((-1, 0, 1), repeat=3) if o != (0, 0, 0)),
    key=lambda o: -(abs(o[0]) + abs(o[1]) + abs(o[2])),
)
WIDE = sorted(
    (o for o in itertools.product(range(NX), (-1, 0, 1), (-1, 0, 1)) if o != (0, 0, 0)),
    key=lambda o: -((o[0] != 0) + (o[0] == 2) + abs(o[1]) + abs(o[2])),
)
CHIPS = sorted(
    (o for o in itertools.product((0,), range(NY), range(0, NZ, 2)) if o != (0, 0, 0)),
    key=lambda o: -(min(o[1], NY - o[1]) + min(o[2], NZ - o[2]) // 2),
)

def side(d):
    return 0 if d < 0 else 1


def constants():
    theta, delta = 0.5 * (CHEB_HIGH + CHEB_LOW), 0.5 * (CHEB_HIGH - CHEB_LOW)
    sigma = theta / delta
    rho, out = np.float32(1.0 / sigma), []
    for _ in range(CHEB - 1):
        rho_next = np.float32(1.0 / (2.0 * sigma - rho))
        out += [np.float32(rho_next * rho), np.float32(2.0 * rho_next / delta)]
        rho = rho_next
    return np.array(out, np.float32), theta


def lane(shape):
    return lax.broadcasted_iota(jnp.int32, shape, len(shape) - 1)


def roll(x, by):
    return pltpu.roll(x, by % 128, x.ndim - 1)


def mm(x, m):
    rows = x.shape[0]
    high = x.astype(jnp.bfloat16)
    rest = x - high.astype(F32)
    mid = rest.astype(jnp.bfloat16)
    low = (rest - mid.astype(F32)).astype(jnp.bfloat16)
    terms = jnp.concatenate([high, mid, low], axis=0)
    out = lax.dot_general(terms, m, (((1,), (0,)), ((), ())), preferred_element_type=F32)
    return out[0:rows] + out[rows : 2 * rows] + out[2 * rows :]


def picks(condition, width=128, value=1.0):
    row = lax.broadcasted_iota(jnp.int32, (128, width), 0)
    col = lax.broadcasted_iota(jnp.int32, (128, width), 1)
    return jnp.where(condition(row, col), F32(value), F32(0.0)).astype(jnp.bfloat16)


def vm(*shape):
    return pltpu.VMEM(shape, F32)


def dma(*shape):
    return pltpu.SemaphoreType.DMA(shape)


def build_scratch():
    s = {}
    for name in ("C0", "V0", "V1", "X0", "VP", "VQ"):
        s[name] = vm(18, 48, 128)
    s.update(WX0=vm(17, 32, 128), WY0=vm(16, 40, 128))
    for name in ("WZM0", "WZP0", "D0", "SD0"):
        s[name] = vm(16, 32, 128)
    s.update(
        YB=vm(2, 5, 16, 1, 128), PZ=vm(5, 32, 128),
        RX=vm(5, 2, 32, 128), RY=vm(2, 5, 16, 1, 128), RZ=vm(2, 5, 32, 128), MZ=vm(5, 32, 128),
        ss=dma(42), rs=dma(42), W=vm(92, 8, 128), hs=dma(8), GV=vm(16, 32, 128), OV=vm(16, 32, 128),
    )
    s.update(RS0=vm(8, 32, 128), RS1=vm(4, 24, 128), RS2=vm(8, 16, 128), QS=vm(4, 16, 128))
    for k, h in (("c", 5), ("g", 4)):
        s["B1" + k] = vm(8, 16, 128)
        s["PZ1" + k] = vm(16, 128)
        s["RX1" + k] = vm(2, h, 16, 128)
        s["RY1" + k] = vm(2, 9, 8, 128)
        s["RE1" + k] = vm(2, 2, h + 1, 8, 128)
        s["RZ1" + k] = vm(2, 3, 3, 16, 128)
        s["ZS" + k] = vm(3, 40, 128)
        s["PB2" + k] = vm(8, 128)
        s["S2" + k] = vm(NX, 3, 3, 8, 128)
        s["PB3" + k] = vm(8, 128)
        s["S3" + k] = vm(8, 128)
        s["YS" + k] = vm(8, 128)
        s["S4" + k] = vm(NY, NZ // 2, 8, 128)
    for l in ("1", "2"):
        for name in ("C", "G", "EA", "EB"):
            s[name + l] = vm(18, 40, 128)
        s.update({"WX" + l: vm(17, 24, 128), "WY" + l: vm(16, 32, 128)})
        for name in ("WZM", "WZP", "D", "SD"):
            s[name + l] = vm(16, 24, 128)
    s["wrap"] = pltpu.SemaphoreType.REGULAR((3,))
    s["K"] = pltpu.SMEM((2 * (CHEB - 1),), F32)
    s.update(U2=vm(20, 24, 128), T21=vm(8, 24, 128), D21=vm(8, 32, 128))
    s.update(TA=vm(10, 24, 128), TB=vm(10, 24, 128), DA=vm(10, 48, 128), DB=vm(10, 32, 128))
    s.update(C3=vm(10, 48, 128), T3=vm(8, 40, 128), KA=vm(10, 48, 128), KB=vm(10, 48, 128), ST3=vm(8, 32, 128))
    s.update(WX3=vm(9, 32, 128), WY3=vm(8, 40, 128))
    for name in ("WXM3", "WXP3", "WYM3", "WYP3", "WZM3", "WZP3", "D3", "SD3"):
        s[name] = vm(8, 32, 128)
    s.update(G3=vm(10, 8, 4, 128), R3=vm(8, 16, 128), T32=vm(8, 16, 128), D32=vm(8, 32, 128))
    return s


def kernel(g_hbm, c_hbm, v_hbm, o_ref, s):
    gx, gy, gz = (lax.axis_index(a) for a in ("gx", "gy", "gz"))
    here = {
        0: {-1: gx > 0, 1: gx < NX - 1},
        1: {-1: gy > 0, 1: gy < NY - 1},
        2: {-1: gz > 0, 1: gz < NZ - 1},
    }
    core = lax.rem(gz, 2)
    started, taken = [], {}

    def exists(o, axes=(0, 1, 2)):
        cond = None
        for axis in axes:
            if o[axis]:
                cond = here[axis][o[axis]] if cond is None else cond & here[axis][o[axis]]
        return cond

    def keep(x, *o, axes=(0, 1, 2)):
        cond = exists(o, axes)
        return x if cond is None else jnp.where(cond, x, 0.0)

    def when(cond, act):
        if cond is None:
            act()
        else:
            pl.when(cond)(act)

    def target(o):
        return (lax.rem(gx + o[0] + NX, NX), lax.rem(gy + o[1] + NY, NY), lax.rem(gz + o[2] + NZ, NZ))

    def send(src, dst, group, o, axes=(0, 1, 2), to=None):
        at = taken.setdefault(group, len(taken))
        copy = pltpu.make_async_remote_copy(
            src_ref=src, dst_ref=dst, send_sem=s["ss"].at[at], recv_sem=s["rs"].at[at],
            device_id=target(o) if to is None else to, device_id_type=MESH,
        )
        out = exists(o, axes)
        when(out, copy.start)
        return group, copy, out, exists(tuple(-d for d in o), axes), int(np.prod(src.shape)) // 1024

    def grouped(copies):
        groups = {}
        for group, copy, out, back, tiles in copies:
            groups.setdefault(group, []).append((copy, out, back, tiles))
        waits = []
        for group, members in groups.items():
            copy, out, back, tiles = members[0]
            if len(members) > 1:
                at, part = taken[group], s["W"].at[pl.ds(0, sum(m[3] for m in members))]
                copy = pltpu.make_async_remote_copy(
                    src_ref=part, dst_ref=part, send_sem=s["ss"].at[at], recv_sem=s["rs"].at[at],
                    device_id=target((0, 0, 1)), device_id_type=MESH,
                )
            started.append((copy, out))
            waits.append((copy, back))
        return waits

    def edges(o):
        axis = next(i for i in range(3) if o[i])
        return jnp.logical_not(here[axis][o[axis]]), s["wrap"], axis

    def tell_edges():
        for o in SIX:
            cond, sem, axis = edges(o)
            when(cond, lambda: pl.semaphore_signal(
                sem.at[axis], inc=1, device_id=target(o), device_id_type=MESH))

    def hear_edges():
        for o in SIX:
            cond, sem, axis = edges(o)
            when(cond, lambda: pl.semaphore_wait(sem.at[axis], 1))

    def arrive(copies):
        for copy, cond in copies:
            when(cond, copy.wait_recv)

    barrier = pltpu.get_barrier_semaphore()
    for o in SIX:
        pl.semaphore_signal(barrier, inc=1, device_id=target(o), device_id_type=MESH)
    main = (pl.ds(1, 16), pl.ds(8, 32))
    loads = [
        pltpu.make_async_copy(c_hbm, s["C0"].at[main], s["hs"].at[0]),
        pltpu.make_async_copy(v_hbm, s["V0"].at[main], s["hs"].at[1]),
        pltpu.make_async_copy(g_hbm, s["GV"], s["hs"].at[2]),
    ]
    for load in loads:
        load.start()

    def pack_fine(plane, k, p, acc):
        s["YB"][0, k, p] = plane[0:1]
        s["YB"][1, k, p] = plane[31:32]
        at = lane((32, 128))
        mine = (at == (2 * p) % 128) | (at == (2 * p - 1) % 128)
        return jnp.where(mine, roll(plane, 2 * p), acc)

    def send_fine(names, k):
        out = []
        yb, rx, ry, rz, pz = s["YB"], s["RX"], s["RY"], s["RZ"], s["PZ"]
        ks = pl.ds(k, len(names))
        out.append(send(yb.at[1, ks], ry.at[0, ks], (k, 0), (0, 1, 0)))
        out.append(send(yb.at[0, ks], ry.at[1, ks], (k, 1), (0, -1, 0)))
        for i, name in enumerate(names):
            low, high = s[name].at[1, pl.ds(8, 32)], s[name].at[16, pl.ds(8, 32)]
            out.append(send(high, rx.at[k + i, 0], (k, 2), (1, 0, 0)))
            out.append(send(low, rx.at[k + i, 1], (k, 3), (-1, 0, 0)))
        out.append(send(pz.at[ks], rz.at[0, ks], (k, 4), (0, 0, 1)))
        out.append(send(pz.at[ks], rz.at[1, ks], (k, 5), (0, 0, -1)))
        return grouped(out)

    def take_fine(name, k):
        v = s[name]
        v[0, 8:40, :] = keep(s["RX"][k, 0], -1, 0, 0)
        v[17, 8:40, :] = keep(s["RX"][k, 1], 1, 0, 0)
        v[1:17, 7:8, :] = keep(s["RY"][0, k], 0, -1, 0)
        v[1:17, 40:41, :] = keep(s["RY"][1, k], 0, 1, 0)
        odd = lane((32, 128)) % 2 == 1
        right, left = keep(s["RZ"][1, k], 0, 0, 1), keep(s["RZ"][0, k], 0, 0, -1)
        s["MZ"][k] = jnp.where(odd, roll(right, -1), roll(left, 1))

    def fine_z(k, extra=None):
        def get(p, v):
            at = lane((32, 128))
            edge = roll(s["MZ"][k], -2 * p)
            if extra is not None:
                edge = edge + extra(p)
            return jnp.where(at == 0, edge, roll(v, 1)), jnp.where(at == 127, edge, roll(v, -1))

        return get

    def plain_z(p, v):
        return roll(v, 1), roll(v, -1)

    def closed_z(p, v):
        at = lane(v.shape)
        return jnp.where(at == 0, 0.0, roll(v, 1)), jnp.where(at == 127, 0.0, roll(v, -1))

    def weights(l, n, rows, scale, zs):
        c, wx, wy = s["C" + l], s["WX" + l], s["WY" + l]
        h = F32(0.5 * scale)
        for p in range(n + 1):
            wx[p] = h * (c[p, 8 : 8 + rows, :] + c[p + 1, 8 : 8 + rows, :])
        for p in range(n):
            wy[p] = h * (c[p + 1, 8 : 16 + rows, :] + c[p + 1, 7 : 15 + rows, :])
            mid = c[p + 1, 8 : 8 + rows, :]
            zm, zp = zs(p, mid)
            wzm, wzp = h * (mid + zm), h * (mid + zp)
            d = wx[p] + wx[p + 1] + wy[p, 0:rows] + wy[p, 1 : rows + 1] + wzm + wzp
            s["WZM" + l][p], s["WZP" + l][p], s["D" + l][p] = wzm, wzp, d
            s["SD" + l][p] = jnp.where(mid > 0, F32(OMEGA) / d, 0.0)

    def gathered(l, v, p, rows, right, zs, skip=0):
        wx, wy = s["WX" + l], s["WY" + l]
        lo, hi, up, here_ = 8 + skip, 8 + skip + rows, slice(skip + 1, skip + rows + 1), slice(skip, skip + rows)
        mid = v[p + 1, lo:hi, :]
        zm, zp = zs(p, mid)
        total = right + wx[p, here_] * v[p, lo:hi, :] + wx[p + 1, here_] * v[p + 2, lo:hi, :]
        total = total + wy[p, here_] * v[p + 1, lo - 1 : hi - 1, :]
        total = total + wy[p, up] * v[p + 1, lo + 1 : hi + 1, :]
        total = total + s["WZM" + l][p, here_] * zm + s["WZP" + l][p, here_] * zp
        return mid, total

    def swept(l, v, p, rows, right, zs):
        mid, total = gathered(l, v, p, rows, right, zs)
        return mid * F32(1.0 - OMEGA) + s["SD" + l][p] * total

    def residual(l, v, p, rows, right, zs, skip=0):
        mid, total = gathered(l, v, p, rows, right, zs, skip)
        return total - s["D" + l][p, skip : skip + rows] * mid

    to_one = picks(lambda r, c: r // 2 + 32 == c, value=0.125)
    to_two = picks(lambda r, c: (c < 32) & (r // 2 == c + 16), value=0.125)
    to_three = picks(lambda r, c: (c // 16 == core) & (r // 2 == c % 16 + 16), value=0.125)

    def side_by_side(x, m):
        out = mm(x.reshape(32, 128), m)
        return out[0:8] + roll(out[8:16], 32) + roll(out[16:24], 64) + roll(out[24:32], 96)

    def restrict_fine(plane, k):
        rs = s["RS0"]
        for q in range(8):
            rs[q] = plane(2 * q) + plane(2 * q + 1)
        half = rs[:, pl.ds(0, 16, stride=2), :] + rs[:, pl.ds(1, 16, stride=2), :]
        block = mm(half.reshape(128, 128), to_one).reshape(8, 16, 128)
        s["B1" + k][...] = block
        at = lane((16, 128))
        acc = jnp.zeros((16, 128), F32)
        for p in range(8):
            acc = jnp.where((at >= 16 * p) & (at < 16 * p + 8), roll(block[p], 16 * p - 32), acc)
            acc = jnp.where((at >= 16 * p + 8) & (at < 16 * p + 16), roll(block[p], 16 * p + 8 - 88), acc)
        s["PZ1" + k][...] = acc

    def restrict_one(plane, first, k):
        rs = s["RS1"]
        rows = 24 if first == 4 else 16
        for q in range(4):
            rs[q, 0:rows] = plane(2 * q) + plane(2 * q + 1)
        half = rs[:, pl.ds(first, 8, stride=2), :] + rs[:, pl.ds(first + 1, 8, stride=2), :]
        s["PB2" + k][...] = side_by_side(half, to_two)

    def restrict_two(plane, k):
        rs, qs = s["RS2"], s["QS"]
        for q in range(8):
            rs[q, 0:8] = plane(2 * q) + plane(2 * q + 1)
        half = rs[:, pl.ds(0, 4, stride=2), :] + rs[:, pl.ds(1, 4, stride=2), :]
        for q in range(4):
            qs[q, 0:4] = half[2 * q]
            qs[q, 4:8] = half[2 * q + 1]
        s["PB3" + k][...] = side_by_side(qs[:, 0:8, :], to_three)

    def send_one(k, h, axes=(0, 1)):
        out = []
        b, pz = s["B1" + k], s["PZ1" + k]
        for i, (dx, dy, dz) in enumerate(AROUND):
            if dz:
                src, dst = pz, s["RZ1" + k].at[side(-dz), 1 - dx, 1 - dy]
            else:
                xs = pl.ds(8 - h, h) if dx > 0 else pl.ds(0, h)
                ys = pl.ds(8, 8) if dy > 0 else pl.ds(0, 8)
                if dx and dy:
                    src, dst = b.at[xs, ys], s["RE1" + k].at[side(-dx), side(-dy), pl.ds(0, h)]
                elif dx:
                    src, dst = b.at[xs], s["RX1" + k].at[side(-dx)]
                else:
                    src, dst = b.at[:, ys], s["RY1" + k].at[side(-dy), pl.ds(0, 8)]
            out.append(send(src, dst, ("one", k, (dx, dy) if axes else 0), (dx, dy, dz), axes))
        return grouped(out)

    def take_one(e, k, h, copies):
        arrive(copies)
        b, rx, ry, re, rz, zs = (s[n + k] for n in ("B1", "RX1", "RY1", "RE1", "RZ1", "ZS"))
        first = lane((16, 128)) % 16 >= 8

        def beside(dx, dy):
            left = keep(rz[0, 1 + dx, 1 + dy], dx, dy, -1)
            right = roll(keep(rz[1, 1 + dx, 1 + dy], dx, dy, 1), 80)
            return jnp.where(first, left, right)

        for dx in (-1, 0, 1):
            zs[1 + dx, 12:28] = beside(dx, 0)
            zs[1 + dx, 12 - h : 12] = beside(dx, -1)[16 - h : 16]
            zs[1 + dx, 28 : 28 + h] = beside(dx, 1)[0:h]
            count, base, start = (8, 5, 0) if dx == 0 else ((h, 5 - h, 8 - h) if dx < 0 else (h, 13, 0))
            planes = pl.ds(base, count)
            if dx == 0:
                e[planes, 12:28, :] = b[...]
                e[planes, 12 - h : 12, :] = keep(ry[0, 0:8, 8 - h : 8, :], 0, -1, 0)
                e[planes, 28 : 28 + h, :] = keep(ry[1, 0:8, 0:h, :], 0, 1, 0)
            else:
                e[planes, 12:28, :] = keep(rx[side(dx)], dx, 0, 0)
                e[planes, 12 - h : 12, :] = keep(re[side(dx), 0, 0:h, 8 - h : 8, :], dx, -1, 0)
                e[planes, 28 : 28 + h, :] = keep(re[side(dx), 1, 0:h, 0:h, :], dx, 1, 0)
            lo, hi = (8, 32) if h == 4 else (0, 40)
            at = lane((hi - lo, 128))
            halo = ((at >= 24) & (at < 32)) | ((at >= 96) & (at < 104))
            for i in range(count):
                moved = roll(zs[1 + dx, lo:hi], 16 - 16 * (start + i))
                e[base + i, lo:hi, :] = jnp.where(halo, moved, e[base + i, lo:hi, :])

    def send_two(k, axes=(1,)):
        out = []
        for i, (a, dy, dz) in enumerate(WIDE):
            dst = s["S2" + k].at[gx, 1 - dy, 1 - dz]
            out.append(send(s["PB2" + k], dst, ("two", k, dy if axes else 0), (a, dy, dz), axes))
        s["S2" + k][gx, 1, 1] = s["PB2" + k][...]
        return grouped(out)

    def take_two(e, k, copies):
        arrive(copies)
        at = lane((8, 128)) // 32
        for x in range(NX):
            for dy in (-1, 0, 1):
                blocks = [keep(s["S2" + k][x, 1 + dy, 1 + dz], 0, dy, dz) for dz in (-1, 0, 1)]
                for p in range(4):
                    val = jnp.zeros((8, 128), F32)
                    for z in range(3):
                        val = jnp.where(at == z, roll(blocks[z], 32 * (z - p)), val)
                    e[1 + 4 * x + p, 16 + 8 * dy : 24 + 8 * dy, :] = val

    def send_core(k):
        to = (gx, gy, gz + 1 - 2 * core)
        return grouped([send(s["PB3" + k], s["S3" + k], ("core", k), (0, 0, 0), to=to)])

    def send_chips(k, copies):
        arrive(copies)
        s["YS" + k][...] = s["PB3" + k][...] + s["S3" + k][...]
        out = []
        for i, o in enumerate(CHIPS):
            dst = s["S4" + k].at[gy, gz // 2]
            out.append(send(s["YS" + k], dst, ("chips", k), o, ()))
        s["S4" + k][gy, gz // 2] = s["YS" + k][...]
        return grouped(out)

    def take_coarse(dst, base, row, k, copies):
        arrive(copies)
        at = lane((8, 128)) // 32
        for g in range(NY):
            for q in range(4):
                val = jnp.zeros((8, 128), F32)
                for j in range(NZ // 2):
                    val = jnp.where(at == j, roll(s["S4" + k][g, j], 32 * (j - q)), val)
                rows = slice(row + 4 * g, row + 4 * g + 4)
                dst[base + 2 * q, rows, :] = val[0:4]
                dst[base + 2 * q + 1, rows, :] = val[4:8]

    for k, name in ((0, "C0"), (1, "V0")):
        loads[k].wait()
        acc = jnp.zeros((32, 128), F32)
        for p in range(16):
            acc = pack_fine(s[name][p + 1, 8:40, :], k, p, acc)
        s["PZ"][k] = acc
    pl.semaphore_wait(barrier, len(SIX))

    copies = send_fine(("C0", "V0"), 0)
    tell_edges()
    loads[2].wait()
    g_ref = s["GV"]
    for name in ("C1", "G1", "EA1", "EB1", "C2", "G2", "EA2", "EB2"):
        s[name][...] = jnp.zeros((18, 40, 128), F32)
    for name in ("C3", "KA", "KB"):
        s[name][...] = jnp.zeros((10, 48, 128), F32)
    s["ZSc"][...] = jnp.zeros((3, 40, 128), F32)
    s["U2"][...] = jnp.zeros((20, 24, 128), F32)
    s["R3"][...] = jnp.zeros((8, 16, 128), F32)
    s["G3"][...] = jnp.zeros((10, 8, 4, 128), F32)
    restrict_fine(lambda p: s["C0"][p + 1, 8:40, :], "c")
    restrict_one(lambda p: s["B1c"][p], 0, "c")
    arrive(copies)
    hear_edges()
    take_fine("C0", 0)
    weights("0", 16, 32, 1.0, fine_z(0))
    take_fine("V0", 1)

    def sweep_fine(src, dst, zs, k):
        acc = jnp.zeros((32, 128), F32)
        for p in range(16):
            new = swept("0", s[src], p, 32, g_ref[p], zs)
            s[dst][p + 1, 8:40, :] = new
            acc = pack_fine(new, k, p, acc)
        s["PZ"][k] = acc
        return send_fine((dst,), k)

    copies = sweep_fine("V0", "V1", fine_z(1), 2)
    tell_edges()
    arrive(copies)
    hear_edges()
    take_fine("V1", 2)
    copies = sweep_fine("V1", "X0", fine_z(2), 3)
    tell_edges()
    c_one = send_one("c", 5, ())
    arrive(copies)
    hear_edges()
    take_fine("X0", 3)
    restrict_fine(lambda p: residual("0", s["X0"], p, 32, g_ref[p], fine_z(3)), "g")

    g_one = send_one("g", 4)
    take_one(s["C1"], "c", 5, c_one)
    c_two = send_two("c", ())
    weights("1", 16, 24, 0.25, plain_z)
    take_one(s["G1"], "g", 4, g_one)

    def begin(l, planes=range(16)):
        for p in planes:
            s["EA" + l][p + 1, 8:32, :] = s["SD" + l][p] * s["G" + l][p + 1, 8:32, :]

    def sweep(l, src, dst, planes=range(16)):
        for p in planes:
            right = s["G" + l][p + 1, 8:32, :]
            s[dst][p + 1, 8:32, :] = swept(l, s[src], p, 24, right, plain_z)

    def left(l, src):
        return lambda p: residual(l, s[src], p, 24, s["G" + l][p + 1, 8:32, :], plain_z)

    begin("1")
    sweep("1", "EA1", "EB1", range(1, 15))
    rest = left("1", "EB1")
    restrict_one(lambda p: rest(p + 4), 4, "g")

    g_two = send_two("g")
    take_two(s["C2"], "c", c_two)
    restrict_two(lambda p: s["C2"][p + 1, 16:24, :], "c")
    c_core = send_core("c")
    weights("2", 16, 24, 0.0625, plain_z)
    c_chips = send_chips("c", c_core)
    take_two(s["G2"], "g", g_two)
    begin("2")
    sweep("2", "EA2", "EB2")
    restrict_two(lambda p: residual("2", s["EB2"], p, 8, s["G2"][p + 1, 16:24, :], plain_z, 8), "g")

    for i, value in enumerate(constants()[0]):
        s["K"][i] = F32(value)
    g_core = send_core("g")
    g_chips = send_chips("g", g_core)
    take_coarse(s["C3"], 1, 8, "c", c_chips)
    weights("3", 8, 32, 0.015625, closed_z)
    at = lane((32, 128))
    for p in range(8):
        inv = F32(1.0) / s["D3"][p]
        s["SD3"][p] = inv
        s["WXM3"][p] = s["WX3"][p] * inv
        s["WXP3"][p] = s["WX3"][p + 1] * inv
        s["WYM3"][p] = s["WY3"][p, 0:32] * inv
        s["WYP3"][p] = s["WY3"][p, 1:33] * inv
        s["WZM3"][p] = jnp.where(at == 0, 0.0, s["WZM3"][p] * inv)
        s["WZP3"][p] = jnp.where(at == 127, 0.0, s["WZP3"][p] * inv)
    take_coarse(s["T3"], 0, 0, "g", g_chips)
    theta = constants()[1]
    for p in range(8):
        t = s["T3"][p, 0:32, :] * s["SD3"][p]
        s["T3"][p, 0:32, :] = t
        d = t * F32(1.0 / theta)
        s["ST3"][p] = d
        s["KA"][p + 1, 8:40, :] = d

    def cheb(src, dst, i):
        a, b = s["K"][2 * i], s["K"][2 * i + 1]
        v = s[src]
        for p in range(8):
            e = v[p + 1, 8:40, :]
            r = s["T3"][p, 0:32, :] - e + s["WXM3"][p] * v[p, 8:40, :] + s["WXP3"][p] * v[p + 2, 8:40, :]
            r = r + s["WYM3"][p] * v[p + 1, 7:39, :] + s["WYP3"][p] * v[p + 1, 9:41, :]
            r = r + s["WZM3"][p] * roll(e, 1) + s["WZP3"][p] * roll(e, -1)
            d = a * s["ST3"][p] + b * r
            s["ST3"][p] = d
            s[dst][p + 1, 8:40, :] = e + d

    def two(i, carry):
        cheb("KA", "KB", 2 * i)
        cheb("KB", "KA", 2 * i + 1)
        return carry

    lax.fori_loop(0, (CHEB - 1) // 2, two, 0)
    cheb("KA", "KB", CHEB - 2)

    for g in range(NY):
        s["G3"][g + 1] = s["KB"][1:9, 8 + 4 * g : 12 + 4 * g, :]
    for j in range(3):
        s["R3"][:, 4 * j : 4 * j + 4, :] = s["G3"][gy + j]
    from_three = picks(lambda r, c: (r == 16 * gz - 16 + c // 2) & (c < 96))
    s["T32"][...] = mm(s["R3"][...].reshape(128, 128), from_three).reshape(8, 16, 128)
    for o in (0, 1):
        s["D32"][:, pl.ds(o, 12, stride=2), :] = s["T32"][:, 0:12, :]
    for p in range(16):
        s["EA2"][p + 1, 8:32, :] = s["EB2"][p + 1, 8:32, :] + s["D32"][p // 2, 0:24, :]
    sweep("2", "EA2", "EB2")
    for p in range(16):
        right = s["G2"][p + 1, 8:32, :]
        s["U2"][p + 2] = swept("2", s["EB2"], p, 24, right, plain_z)

    from_two = picks(lambda r, c: (r == 16 + c // 2) & (c >= 24) & (c < 104))
    part = s["U2"][pl.ds(4 * gx, 8)]
    s["T21"][...] = mm(part.reshape(192, 128), from_two).reshape(8, 24, 128)
    for o in (0, 1):
        s["D21"][:, pl.ds(o, 12, stride=2), :] = s["T21"][:, 6:18, :]
    for p in range(1, 15):
        s["EA1"][p + 1, 8:32, :] = s["EB1"][p + 1, 8:32, :] + s["D21"][p // 2, 0:24, :]
    sweep("1", "EA1", "EB1", range(2, 14))
    sweep("1", "EB1", "EA1", range(3, 13))

    from_one = picks(
        lambda r, c: ((c < 128) & (r == 32 + c // 2)) | ((c == 128) & (r == 31)) | ((c == 255) & (r == 96)), 256
    )
    wide = mm(s["EA1"][4:14, 8:32, :].reshape(240, 128), from_one)
    s["TA"][...] = wide[:, 0:128].reshape(10, 24, 128)
    s["TB"][...] = wide[:, 128:256].reshape(10, 24, 128)
    for o in (0, 1):
        s["DA"][:, pl.ds(8 + o, 16, stride=2), :] = s["TA"][:, 4:20, :]
        s["DB"][:, pl.ds(o, 16, stride=2), :] = s["TB"][:, 4:20, :]
    for i in range(18):
        j = (i + 1) // 2
        s["VP"][i, 8:40, :] = s["X0"][i, 8:40, :] + s["DA"][j, 8:40, :]
        if 0 < i < 17:
            s["VP"][i, 7:8, :] = s["X0"][i, 7:8, :] + s["TA"][j, 3:4, :]
            s["VP"][i, 40:41, :] = s["X0"][i, 40:41, :] + s["TA"][j, 20:21, :]
    earlier = len(started)
    copies = sweep_fine("VP", "VQ", fine_z(3, lambda p: s["DB"][(p + 2) // 2]), 4)
    for copy, cond in started[:earlier]:
        when(cond, copy.wait_send)
    arrive(copies)
    take_fine("VQ", 4)
    stores = []
    for p in range(16):
        s["OV"][p] = swept("0", s["VQ"], p, 32, g_ref[p], fine_z(4))
        if p % 4 == 3:
            part = pl.ds(p - 3, 4)
            stores.append(pltpu.make_async_copy(s["OV"].at[part], o_ref.at[part], s["hs"].at[3 + p // 4]))
            stores[-1].start()
    for copy, cond in started[earlier:]:
        when(cond, copy.wait_send)
    for copy in stores:
        copy.wait()


def on_device(right_side, coefficient, guess):
    whole = pl.BlockSpec(memory_space=pl.ANY)
    return pl.pallas_call(
        kernel,
        out_shape=jax.ShapeDtypeStruct((16, 32, 128), F32),
        in_specs=[whole, whole, whole],
        out_specs=whole,
        scratch_shapes=[build_scratch()],
        compiler_params=pltpu.CompilerParams(
            collective_id=0, has_side_effects=True, vmem_limit_bytes=56 * 2**20
        ),
    )(right_side, coefficient, guess)


def solution(mesh):
    spec = P("gx", "gy", "gz")
    return jax.shard_map(on_device, mesh=mesh, in_specs=(spec, spec, spec), out_specs=spec, check_vma=False)
```
